128 devices in a mesh: grp: 4 (over x), tp: 32 (over z, y, core).
Axes of the slice: x: 4, y: 4, z: 4, core: 2. Of those that a mesh axis runs over, the one named last changes fastest.
Arguments:
- tokens: bfloat16 [4096, 8192], P('grp', 'tp'), may hold values from -6 to 6
- norm_gain: bfloat16 [8192], P('tp'), may hold values from 0.5 to 1.5
- w_query: bfloat16 [8192, 8192], P(None, 'tp'), may hold values from -0.0625 to 0.0625
- key_value_weight: bfloat16 [8192, 2, 1024], P(None, None, 'tp'), may hold values from -0.0625 to 0.0625
- w_out: bfloat16 [8192, 8192], P('tp'), may hold values from -0.0625 to 0.0625
- doc_lengths: int32 [4, 4], P('grp'), may hold values from 1 to 512, 1024 in all within a row
- holder: int32 [256, 1], replicated, may hold values from 0 to 127; in each aligned block of 64 rows (0 to 63, 64 to 127, ...) at most 2 rows name the same one
Outputs:
- mixed: bfloat16 [4096, 8192], P('grp', 'tp')
- kv_store: bfloat16 [128, 4, 2, 2, 128, 128], P(('grp', 'tp'))
The draws below stay inside these ranges and needn't reach their ends.
Inputs may be any that keep to these rules, and one draw needn't show every extreme that they name: holder names a device by its index over grp and tp together, grp slowest. Within the 64 rows of one group no device is named more than 2 times, and some device exactly 2 times. `doc_lengths`: each row lists whole document lengths summing to 1024.
All inputs are finite; a program needn't handle non-finite values.
Results may differ from the reference program's by a relative error of at most 0.01.
Values may be sent and summed in bfloat16 or wider, within the bound.
No kernel may reach another device: no remote copies, remote signals or barrier semaphores. Data moves between devices by JAX's collectives and lax.ppermute only.
A program may use at most 128 MiB of HBM per device.

```python
import math
import jax
import jax.numpy as jnp
import numpy as np
from jax import lax

MODEL_WIDTH = 8192
QUERY_HEADS = 64
KEY_VALUE_HEADS = 8
HEAD_SIZE = 128
SEQ_DEV = 32
BLOCK_TOKENS = 128
NDOC = 4
HOLD = 2
SEQ = 1024
TOKENS = 4096
NBH = 64
N_GRP = 4
N_TP = 32


def shard_levels(own_key, dims, pieces, low, largest):
    def one(axis_at, blocks):
        draws = jax.random.uniform(jax.random.fold_in(jax.random.fold_in(own_key, 6), axis_at), (blocks,), jnp.float32, low / len(pieces), largest / len(pieces))
        return jnp.repeat(jnp.exp(draws), dims[axis_at] // blocks).reshape((-1,) + (1,) * (len(dims) - axis_at - 1))

    factor_of = one(*pieces[0])
    for cut in pieces[1:]:
        factor_of = factor_of * one(*cut)
    return factor_of


def profile(count, total, reach, slope):
    loads = [(1 << 20) // math.isqrt(grade ** slope) + 1 for grade in range(2, count + 1)]
    spare, given = total - reach - (count - 1), [1] * (count - 1)
    while spare > 0:
        free = [i for i in range(count - 1) if given[i] < reach]
        whole, left = sum([loads[i] for i in free]), spare
        for i in free:
            more = min(reach - given[i], max(1, left * loads[i] // whole), spare)
            given[i] = given[i] + more
            spare = spare - more
    return np.array([reach] + given)


def uneven(stream_key, count, total, bound, skew):
    if count == 2:
        one = jax.random.randint(stream_key, (), max(1, total - bound), min(bound, total - 1) + 1)
        return jnp.stack([one, total - one])
    lengths = jnp.asarray(profile(count, total, bound, skew), jnp.int32)
    twos = (count - 1) // 2
    source_of, sink = lengths[1:1 + 2 * twos:2], lengths[2:2 + 2 * twos:2]
    room = jnp.minimum(source_of - 1, bound - sink)
    moved = jax.random.randint(jax.random.fold_in(stream_key, 1), (twos,), 0, 1 << 20) % (room + 1)
    lengths = lengths.at[1:1 + 2 * twos:2].set(source_of - moved).at[2:2 + 2 * twos:2].set(sink + moved)
    return lengths[jax.random.permutation(jax.random.fold_in(stream_key, 2), count)]


def routed_block(key, own, number, rows, amount, top, reach, slope):
    sequence = jax.random.permutation(key, amount)
    heavy_load, usual = shares(amount, rows * top, reach, slope, True), shares(amount, rows * top, reach, slope, False)
    places = jnp.arange(amount)

    def named(tallies, rotation):
        used = int((tallies > 0).sum())
        fixed = max(1, used // 4)
        moved = fixed + (places - fixed + rotation * (used - fixed)) % max(1, amount - fixed)
        return jnp.zeros((amount,), jnp.int32).at[sequence[jnp.where(places < fixed, places, moved)]].set(jnp.asarray(tallies, jnp.int32))

    tallies = jnp.where(number % 4 == 0, named(heavy_load, number // 4), named(usual, number - number // 4 - 1))
    mixed = jax.random.permutation(jax.random.fold_in(own, 3), amount)
    giver, receiver = mixed[0:amount // 2 * 2:2], mixed[1:amount // 2 * 2:2]
    margin = jnp.minimum(tallies[giver] - 1, reach - tallies[receiver]) // 2
    margin = jnp.where((giver == sequence[0]) | (receiver == sequence[0]) | (tallies[receiver] == 0), 0, jnp.maximum(margin, 0))
    moved = jax.random.randint(jax.random.fold_in(own, 4), (amount // 2,), 0, 1 << 20) % (margin + 1)
    tallies = tallies.at[giver].add(-moved).at[receiver].add(moved)
    members = jnp.searchsorted(jnp.cumsum(tallies), jnp.arange(rows * top), side="right").astype(jnp.int32)
    table = members.reshape(top, rows).T
    table = table[jax.random.permutation(jax.random.fold_in(own, 1), rows)]
    rotation = jax.random.randint(jax.random.fold_in(own, 2), (rows, 1), 0, top)
    return jnp.take_along_axis(table, (jnp.arange(top)[None, :] + rotation) % top, axis=1)


def shares(amount, total, limit, lean, full):
    weights = [(1 << 20) // math.isqrt(standing ** lean) + 1 for standing in range(1, amount + 1)]
    largest = limit if full else min(limit, max(-(-total // amount), total * weights[0] // sum(weights)))
    least = 1 if total - largest >= amount - 1 else 0
    holding, surplus = [largest] + [least] * (amount - 1), total - largest - least * (amount - 1)
    while surplus > 0:
        movable = [i for i in range(1, amount) if holding[i] < largest] or [i for i in range(1, amount) if holding[i] < limit]
        mass, budget = sum([weights[i] for i in movable]), surplus
        for i in movable:
            extra = min(limit - holding[i], max(1, budget * weights[i] // mass), surplus)
            holding[i] = holding[i] + extra
            surplus = surplus - extra
    return np.array(holding)


def scatter_about(rng, extent, spread, reach, split=(), held_as=jnp.bfloat16):
    drawn = jax.random.normal(rng, extent, jnp.float32) * spread
    if len(split) > 0:
        drawn = shard_levels(rng, extent, split, -0.22, 0.18) * drawn
    return jnp.clip(drawn, min=-reach, max=reach).astype(held_as)


def setup_inputs(seed: int = 0) -> dict:
    key_of = jax.random.split(jax.random.key(seed), 8)
    tokens = scatter_about(key_of[0], (TOKENS, MODEL_WIDTH), 1.0, 6.0, ((0, 4), (1, 32)))
    norm_gain = jnp.clip(1.0 + 0.1 * jax.random.normal(key_of[1], (MODEL_WIDTH,), jnp.float32), 0.5, 1.5).astype(jnp.bfloat16)
    w_query = scatter_about(key_of[2], (MODEL_WIDTH, QUERY_HEADS * HEAD_SIZE), MODEL_WIDTH ** -0.5, 0.0625, ((1, 32),))
    key_value_weight = scatter_about(key_of[3], (MODEL_WIDTH, 2, KEY_VALUE_HEADS * HEAD_SIZE), MODEL_WIDTH ** -0.5, 0.0625, ((2, 32),))
    w_out = scatter_about(key_of[4], (QUERY_HEADS * HEAD_SIZE, MODEL_WIDTH), (QUERY_HEADS * HEAD_SIZE) ** -0.5, 0.0625, ((0, 32),))
    doc_lengths = jax.vmap(lambda own: uneven(own, NDOC, SEQ, SEQ // 2, 2))(jax.random.split(key_of[5], N_GRP)).reshape((N_GRP, NDOC)).astype(jnp.int32)
    holder_keys = jax.random.split(jax.random.fold_in(key_of[6], 1), (N_GRP * NBH) // NBH)
    holder_turns = jax.random.permutation(jax.random.fold_in(key_of[6], 3), (N_GRP * NBH) // NBH)
    holder = jax.vmap(lambda own, number: routed_block(jax.random.fold_in(key_of[6], 2), own, number, NBH, N_GRP * N_TP, 1, HOLD, 2))(holder_keys, holder_turns).reshape((N_GRP * NBH, 1))
    return dict(tokens=tokens, norm_gain=norm_gain, w_query=w_query, key_value_weight=key_value_weight, w_out=w_out, doc_lengths=doc_lengths, holder=holder)


rope_base = 500000.0
norm_eps = 1e-05
mask_fill = -1e+30

def doc_starts(lengths_row, sequence_length):
    lengths_int = lengths_row.astype(jnp.int32)
    ends = jnp.cumsum(lengths_int).astype(jnp.int32)
    indices = jnp.arange(sequence_length, dtype=jnp.int32)
    passed = (indices[:, None] >= ends[None, :]).astype(jnp.int32)
    return lax.optimization_barrier(jnp.sum(passed * lengths_int[None, :], axis=1)).astype(jnp.int32)

def rotate(vectors, token_positions):
    half_dim = vectors.shape[-1] // 2
    frequency = jnp.exp(jnp.arange(half_dim, dtype=jnp.float32) * (-2.0 * math.log(rope_base) / vectors.shape[-1]))
    angles = token_positions.astype(jnp.float32)[:, None, None] * frequency[None, None, :]
    cosine = jnp.cos(angles)
    sine = jnp.sin(angles)
    first = vectors[..., :half_dim]
    second = vectors[..., half_dim:]
    return jnp.concatenate([first * cosine - second * sine, second * cosine + first * sine], axis=-1)

def attend(group_queries, key_slice, value_slice, allowed):
    scores = jnp.einsum('hqd,kd->hqk', group_queries.astype(jnp.float32), key_slice.astype(jnp.float32))
    scores = scores * (1.0 / math.sqrt(group_queries.shape[-1]))
    scores = jnp.where(allowed[None], scores, mask_fill)
    peak = lax.optimization_barrier(jnp.max(scores, axis=-1, keepdims=True))
    weights = jnp.exp(scores - peak)
    probs = (weights / lax.optimization_barrier(jnp.sum(weights, axis=-1, keepdims=True))).astype(jnp.bfloat16)
    attention_output = jnp.einsum('hqk,kd->hqd', probs.astype(jnp.float32), value_slice.astype(jnp.float32))
    return attention_output.astype(jnp.bfloat16)

def store_blocks(rotary_keys, value_rows, owners, devices):
    sequence_length = rotary_keys.shape[0]
    head_block_count = sequence_length // BLOCK_TOKENS * KEY_VALUE_HEADS
    paged_blocks = jnp.stack([rotary_keys, value_rows], axis=1).reshape(sequence_length // BLOCK_TOKENS, BLOCK_TOKENS, 2, KEY_VALUE_HEADS, HEAD_SIZE)
    paged_blocks = paged_blocks.transpose(0, 3, 2, 1, 4).reshape(head_block_count, 2, BLOCK_TOKENS, HEAD_SIZE)
    onehot = (owners[:, None] == jnp.arange(devices, dtype=jnp.int32)[None, :]).astype(jnp.int32)
    slot_rank = jnp.cumsum(onehot, axis=0).astype(jnp.int32) - onehot
    chooser = jnp.stack([onehot * (slot_rank == slot).astype(jnp.int32) for slot in range(HOLD)], axis=0)
    stored = jnp.einsum('rbe,bkxd->erkxd', chooser.astype(jnp.float32), paged_blocks.astype(jnp.float32))
    return stored.astype(jnp.bfloat16)

def one_group(tokens, norm_gain, w_query, key_value_weight, w_out, lengths_row, owners):
    sequence_length = tokens.shape[0]
    tok_float = tokens.astype(jnp.float32)
    factor = lax.rsqrt(lax.optimization_barrier(jnp.mean(tok_float * tok_float, axis=1, keepdims=True)) + norm_eps)
    normalized_input = (tok_float * factor * norm_gain.astype(jnp.float32)[None, :]).astype(jnp.bfloat16)
    starts = doc_starts(lengths_row, sequence_length)
    token_positions = jnp.arange(sequence_length, dtype=jnp.int32) - starts
    queries = jnp.dot(normalized_input, w_query, preferred_element_type=jnp.float32).reshape(sequence_length, QUERY_HEADS, HEAD_SIZE)
    queries = rotate(queries, token_positions).astype(jnp.bfloat16)
    key_value_rows = jnp.dot(normalized_input, key_value_weight.reshape(MODEL_WIDTH, 2 * KEY_VALUE_HEADS * HEAD_SIZE), preferred_element_type=jnp.float32)
    key_value_rows = key_value_rows.astype(jnp.bfloat16).reshape(sequence_length, 2, KEY_VALUE_HEADS, HEAD_SIZE)
    rotary_keys = rotate(key_value_rows[:, 0].astype(jnp.float32), token_positions).astype(jnp.bfloat16)
    value_rows = key_value_rows[:, 1]
    indices = jnp.arange(sequence_length, dtype=jnp.int32)
    allowed = (indices[None, :] <= indices[:, None]) & (indices[None, :] >= starts[:, None])
    device_portion = QUERY_HEADS // KEY_VALUE_HEADS

    def key_value_head(head_kv):
        group_queries = lax.dynamic_slice_in_dim(queries, (head_kv * device_portion).astype(jnp.int32), device_portion, 1)
        group_queries = group_queries.transpose(1, 0, 2)
        key_slice = lax.dynamic_index_in_dim(rotary_keys, head_kv, 1, keepdims=False)
        value_slice = lax.dynamic_index_in_dim(value_rows, head_kv, 1, keepdims=False)
        return attend(group_queries, key_slice, value_slice, allowed)
    attention_output = lax.map(key_value_head, jnp.arange(KEY_VALUE_HEADS, dtype=jnp.int32))
    attention_output = attention_output.reshape(QUERY_HEADS, sequence_length, HEAD_SIZE).transpose(1, 0, 2).reshape(sequence_length, QUERY_HEADS * HEAD_SIZE)
    columns = QUERY_HEADS * HEAD_SIZE // N_TP

    def add_part(step_index, total):
        offset = (step_index * columns).astype(jnp.int32)
        part_cols = lax.dynamic_slice_in_dim(attention_output, offset, columns, 1)
        part_rows = lax.dynamic_slice_in_dim(w_out, offset, columns, 0)
        term = jnp.dot(part_cols, part_rows, preferred_element_type=jnp.float32).astype(jnp.bfloat16)
        term = lax.optimization_barrier(term)
        return total + term.astype(jnp.float32)
    summed = lax.fori_loop(0, N_TP, add_part, jnp.zeros((sequence_length, MODEL_WIDTH), jnp.float32))
    mixed = (tok_float + summed).astype(jnp.bfloat16)
    stored = store_blocks(rotary_keys, value_rows, owners, N_GRP * N_TP)
    return (mixed, stored)

def reference(tokens, norm_gain, w_query, key_value_weight, w_out, doc_lengths, holder):
    sequence_length = SEQ_DEV * N_TP
    head_block_count = sequence_length // BLOCK_TOKENS * KEY_VALUE_HEADS
    mixed_parts = []
    stored_parts = []
    for group_index in range(N_GRP):
        group_tokens = tokens[group_index * sequence_length:(group_index + 1) * sequence_length]
        owners = holder[group_index * head_block_count:(group_index + 1) * head_block_count, 0].astype(jnp.int32)
        mixed, stored = one_group(group_tokens, norm_gain, w_query, key_value_weight, w_out, doc_lengths[group_index], owners)
        mixed_parts.append(mixed)
        stored_parts.append(stored)
    return (jnp.concatenate(mixed_parts, axis=0), jnp.stack(stored_parts, axis=1))
```

```python
import functools
import math

import jax
import jax.numpy as jnp
from jax import lax
from jax.experimental import pallas as pl
from jax.experimental.pallas import tpu as pltpu
from jax.sharding import Mesh
from jax.sharding import PartitionSpec as P

WIDTH = 8192
HEAD = 128
BLOCK = 128
SEQ = 1024
COLS = 256
CHUNK = 512
ROPE_BASE = 500000.0
EPS = 1e-05
FILL = -1e30
SCORE_SCALE = math.log2(math.e) / math.sqrt(HEAD)
bf16 = jnp.bfloat16
f32 = jnp.float32

SHIFT = {d: [(i, (i + d) % 4) for i in range(4)] for d in (1, 2, 3)}
SWAP = [(0, 1), (1, 0)]
PAIR = [(0, 1), (1, 0), (2, 3), (3, 2)]


def shift(value, axis, distance):
    return lax.ppermute(value, axis, SHIFT[distance])


def swap(value):
    return lax.ppermute(value, "c", SWAP)


def rotate(vectors, cosine, sine):
    return vectors * cosine + pltpu.roll(vectors, HEAD // 2, 1) * sine


def scale_kernel(tokens, gain, sent):
    tok = tokens[...].astype(f32)
    sent[0:SEQ, :] = (tok * gain[...].astype(f32)).astype(bf16)
    diagonal = lax.broadcasted_iota(jnp.int32, (COLS, COLS), 0) == lax.broadcasted_iota(
        jnp.int32, (COLS, COLS), 1
    )
    rows = []
    for part in range(SEQ // COLS):
        here = tok[part * COLS : (part + 1) * COLS, :]
        column = jnp.sum(here * here, axis=1, keepdims=True)
        rows.append(jnp.sum(jnp.where(diagonal, column, 0.0), axis=0, keepdims=True))
    total = jnp.concatenate(rows + [jnp.zeros((4, COLS), f32)], axis=0)
    high = total.astype(bf16).astype(f32)
    sent[SEQ : SEQ + 16, :] = jnp.concatenate([high, total - high], axis=0).astype(bf16)


def scale_tokens(tokens, gain):
    return pl.pallas_call(
        scale_kernel,
        out_shape=jax.ShapeDtypeStruct((SEQ + 16, COLS), bf16),
        compiler_params=pltpu.CompilerParams(vmem_limit_bytes=56 << 20),
        name="scale_tokens",
    )(tokens, gain.reshape(1, COLS))


def attention_kernel(chunk, steps, per_step, lengths, x, squares, w_q, w_kv, cosine, sine, *rest):
    if chunk == 0:
        attended, keys, values, acc_q, acc_kv, acc_s, all_k, all_v = rest
    else:
        old_k, old_v, attended, keys, values, acc_q, acc_kv, acc_s, all_k, all_v = rest
    step = pl.program_id(0)

    @pl.when(step == 0)
    def _():
        acc_q[...] = jnp.zeros_like(acc_q)
        acc_kv[...] = jnp.zeros_like(acc_kv)
        acc_s[...] = jnp.zeros_like(acc_s)

    rows = jnp.concatenate([x[i] for i in range(per_step)], axis=1)
    acc_q[...] += jnp.dot(rows, w_q[...], preferred_element_type=f32)
    acc_kv[...] += jnp.dot(rows, w_kv[...], preferred_element_type=f32)
    for i in range(per_step):
        acc_s[...] += squares[i].astype(f32)

    @pl.when(step == steps - 1)
    def _():
        base = chunk * CHUNK
        diagonal = lax.broadcasted_iota(jnp.int32, (256, 256), 0) == lax.broadcasted_iota(
            jnp.int32, (256, 256), 1
        )
        for part in range(CHUNK // 256):
            row = (base + part * 256) // 256
            total = acc_s[row : row + 1, :] + acc_s[row + 8 : row + 9, :]
            factor = lax.rsqrt(total * (1.0 / WIDTH) + EPS)
            column = jnp.sum(jnp.where(diagonal, factor, 0.0), axis=1, keepdims=True)
            here = pl.ds(part * 256, 256)
            c, s = cosine[here, :], sine[here, :]
            q = acc_q[here, :] * column
            acc_q[here, :] = jnp.concatenate(
                [rotate(q[:, :HEAD], c, s), rotate(q[:, HEAD:], c, s)], axis=1
            )
            kv = (acc_kv[here, :] * column).astype(bf16)
            k = rotate(kv[:, :HEAD].astype(f32), c, s).astype(bf16)
            keys[here, :] = k
            values[here, :] = kv[:, HEAD:]
            there = pl.ds(base + part * 256, 256)
            all_k[there, :] = k
            all_v[there, :] = kv[:, HEAD:]
        if chunk > 0:
            all_k[0:base, :] = old_k[...]
            all_v[0:base, :] = old_v[...]
        for part in range(CHUNK // 256):
            first = base + part * 256
            low = max(0, first - 512)
            high = first + 256
            here = pl.ds(part * 256, 256)
            i = lax.broadcasted_iota(jnp.int32, (256, 1), 0) + first
            starts = jnp.zeros((256, 1), jnp.int32)
            end = jnp.int32(0)
            for doc in range(4):
                end = end + lengths[doc]
                starts = starts + jnp.where(i >= end, lengths[doc], 0)
            j = lax.broadcasted_iota(jnp.int32, (256, high - low), 1) + low
            allowed = (j <= i) & (j >= starts)
            k = all_k[low:high, :]
            v = all_v[low:high, :]
            outs = []
            for head in range(2):
                q = acc_q[here, head * HEAD : (head + 1) * HEAD].astype(bf16)
                scores = lax.dot_general(q, k, (((1,), (1,)), ((), ())), preferred_element_type=f32)
                scores = jnp.where(allowed, scores * SCORE_SCALE, FILL)
                peak = jnp.max(scores, axis=1, keepdims=True)
                weights = jnp.exp2(scores - peak)
                norm = jnp.sum(weights, axis=1, keepdims=True)
                out = jnp.dot(weights.astype(bf16), v, preferred_element_type=f32)
                outs.append(out / norm)
            attended[here, :] = jnp.concatenate(outs, axis=1).astype(bf16)


def attend_chunk(chunk, gathered, w_q, w_kv, cosine, sine, lengths, old):
    per_step = 4
    steps = 32 // per_step
    in_specs = [
        pl.BlockSpec((per_step, CHUNK, COLS), lambda k, n: (k, chunk, 0)),
        pl.BlockSpec((per_step, 16, COLS), lambda k, n: (k, SEQ // 16, 0)),
        pl.BlockSpec((per_step * COLS, COLS), lambda k, n: (k, 0)),
        pl.BlockSpec((per_step * COLS, COLS), lambda k, n: (k, 0)),
        pl.BlockSpec((CHUNK, HEAD), lambda k, n: (chunk, 0)),
        pl.BlockSpec((CHUNK, HEAD), lambda k, n: (chunk, 0)),
    ]
    args = [gathered, gathered, w_q, w_kv, cosine, sine]
    for part in old:
        in_specs.append(pl.BlockSpec((CHUNK, HEAD), lambda k, n: (0, 0)))
        args.append(part)
    return pl.pallas_call(
        functools.partial(attention_kernel, chunk, steps, per_step),
        grid_spec=pltpu.PrefetchScalarGridSpec(
            num_scalar_prefetch=1,
            grid=(steps,),
            in_specs=in_specs,
            out_specs=[
                pl.BlockSpec((CHUNK, COLS), lambda k, n: (0, 0)),
                pl.BlockSpec((CHUNK, HEAD), lambda k, n: (0, 0)),
                pl.BlockSpec((CHUNK, HEAD), lambda k, n: (0, 0)),
            ],
            scratch_shapes=[
                pltpu.VMEM((CHUNK, COLS), f32),
                pltpu.VMEM((CHUNK, COLS), f32),
                pltpu.VMEM((16, COLS), f32),
                pltpu.VMEM((SEQ, HEAD), bf16),
                pltpu.VMEM((SEQ, HEAD), bf16),
            ],
        ),
        out_shape=[
            jax.ShapeDtypeStruct((CHUNK, COLS), bf16),
            jax.ShapeDtypeStruct((CHUNK, HEAD), bf16),
            jax.ShapeDtypeStruct((CHUNK, HEAD), bf16),
        ],
        compiler_params=pltpu.CompilerParams(vmem_limit_bytes=56 << 20),
        cost_estimate=pl.CostEstimate(
            flops=2 * CHUNK * WIDTH * 512, bytes_accessed=24 << 20, transcendentals=1 << 20
        ),
        name="project_attend",
    )(lengths, *args)


def out_kernel(order, *refs):
    blocks, weights, outs = refs[:8], refs[8], refs[9:]
    step = pl.program_id(0)
    rows = jnp.concatenate([b[...] for b in blocks], axis=1)
    part = jnp.dot(rows, weights[0], preferred_element_type=f32).astype(bf16)
    for i in range(4):

        @pl.when(step == i)
        def _():
            outs[i][...] = part


def project_out(order, blocks, weights):
    whole = pl.BlockSpec((CHUNK, COLS), lambda i, n: (0, 0))
    return pl.pallas_call(
        out_kernel,
        grid_spec=pltpu.PrefetchScalarGridSpec(
            num_scalar_prefetch=1,
            grid=(4,),
            in_specs=[whole] * 8 + [pl.BlockSpec((1, 8 * COLS, COLS), lambda i, n: (n[i], 0, 0))],
            out_specs=[whole] * 4,
        ),
        out_shape=[jax.ShapeDtypeStruct((CHUNK, COLS), bf16)] * 4,
        compiler_params=pltpu.CompilerParams(vmem_limit_bytes=56 << 20),
        cost_estimate=pl.CostEstimate(
            flops=2 * CHUNK * 2048 * 1024, bytes_accessed=8 << 20, transcendentals=0
        ),
        name="project_out",
    )(order, *blocks, weights)


def pick_kernel(index, valid, blocks, *rest):
    outs, sems = rest[:4], rest[4]

    def copy(i):
        return pltpu.make_async_copy(blocks.at[index[i]], outs[i // 2].at[i % 2], sems.at[i])

    for i in range(8):

        @pl.when(valid[i] > 0)
        def _():
            copy(i).start()

        @pl.when(valid[i] <= 0)
        def _():
            outs[i // 2][i % 2] = jnp.zeros((2, BLOCK, HEAD), bf16)

    for i in range(8):

        @pl.when(valid[i] > 0)
        def _():
            copy(i).wait()


def pick_blocks(index, valid, blocks):
    shape = (2, 2, BLOCK, HEAD)
    return pl.pallas_call(
        pick_kernel,
        grid_spec=pltpu.PrefetchScalarGridSpec(
            num_scalar_prefetch=2,
            grid=(1,),
            in_specs=[pl.BlockSpec(memory_space=pl.ANY)],
            out_specs=[pl.BlockSpec(shape, lambda i, n, m: (0, 0, 0, 0))] * 4,
            scratch_shapes=[pltpu.SemaphoreType.DMA((8,))],
        ),
        out_shape=[jax.ShapeDtypeStruct(shape, bf16)] * 4,
        compiler_params=pltpu.CompilerParams(vmem_limit_bytes=56 << 20),
        cost_estimate=pl.CostEstimate(flops=0, bytes_accessed=2 << 20, transcendentals=0),
        name="pick_blocks",
    )(index, valid, blocks)


def spread_out_weights(w_out, g, y, c):
    def piece(d):
        column = (g * 8 + ((y + d) % 4) * 2) * COLS
        return lax.dynamic_slice(w_out, (0, column), (COLS, 2 * COLS))

    parts = [piece(0)] + [shift(piece(d), "y", d) for d in (1, 2, 3)]
    mine = jnp.stack([lax.dynamic_slice(p, (0, c * COLS), (COLS, COLS)) for p in parts])
    send = jnp.stack([lax.dynamic_slice(p, (0, (1 - c) * COLS), (COLS, COLS)) for p in parts])
    theirs = swap(send)
    local = jnp.stack([mine, theirs], axis=1).reshape(8 * COLS, COLS)
    return jnp.stack([local] + [shift(local, "g", d) for d in (1, 2, 3)])


def head_weights(kv_weight, y, c):
    own = kv_weight.transpose(1, 2, 0)
    near = lax.ppermute(own, "y", PAIR)
    both = jnp.where(y % 2 == 0, jnp.stack([own, near]), jnp.stack([near, own]))
    other = swap(both)
    cores = jnp.where(c == 0, jnp.stack([both, other], 1), jnp.stack([other, both], 1))
    return cores.transpose(4, 2, 0, 1, 3).reshape(WIDTH, 2 * HEAD)


def rope_tables(lengths):
    ends = jnp.cumsum(lengths)
    i = jnp.arange(SEQ, dtype=jnp.int32)
    passed = (i[:, None] >= ends[None, :]).astype(jnp.int32)
    positions = (i - jnp.sum(passed * lengths[None, :], axis=1)).astype(f32)
    frequency = jnp.exp(jnp.arange(HEAD // 2, dtype=f32) * (-2.0 * math.log(ROPE_BASE) / HEAD))
    angles = positions[:, None] * frequency[None, :]
    cosine, sine = jnp.cos(angles), jnp.sin(angles)
    return jnp.concatenate([cosine, cosine], 1), jnp.concatenate([-sine, sine], 1)


def store_plan(holder, g, z, y, c):
    owners = lax.dynamic_slice(holder[:, 0], (g * 64,), (64,))
    same = owners[:, None] == owners[None, :]
    before = jnp.arange(64)[None, :] < jnp.arange(64)[:, None]
    rank = jnp.sum((same & before).astype(jnp.int32), axis=1)
    slots = jnp.arange(64, dtype=jnp.int32)
    z_of, y_of, rest = slots // 16, (slots // 4) % 4, slots % 4
    block = ((y_of % 2) * 4 + rest) * 8 + z_of * 2 + y_of // 2
    owner, slot = owners[block], rank[block]
    target = (((g + jnp.arange(4)) % 4) * 32 + z * 8 + y * 2 + c).astype(jnp.int32)
    hit = (owner[None, None, :] == target[:, None, None]) & (
        slot[None, None, :] == jnp.arange(2)[None, :, None]
    )
    hit = hit.reshape(8, 64).astype(jnp.int32)
    return jnp.sum(hit * slots[None, :], axis=1), jnp.sum(hit, axis=1)


def local(tokens, norm_gain, w_query, kv_weight, w_out, doc_lengths, holder):
    g, z, y, c = (lax.axis_index(a) for a in ("g", "z", "y", "c"))
    sent = scale_tokens(tokens, norm_gain)
    gathered = lax.all_gather(sent, ("z", "y", "c"))

    lengths = doc_lengths[0]
    cosine, sine = rope_tables(lengths)
    w_kv = head_weights(kv_weight, y, c)
    w_o = spread_out_weights(w_out, g, y, c)
    order = jnp.stack([(g - z - d) % 4 for d in range(4)]).astype(jnp.int32)
    index, valid = store_plan(holder, g, z, y, c)

    gathered, w_kv, w_o, index, valid, cosine, sine = lax.optimization_barrier(
        (gathered, w_kv, w_o, index, valid, cosine, sine)
    )
    old = ()
    sums, keys, values = [], [], []
    for chunk in range(SEQ // CHUNK):
        attended, k, v = attend_chunk(chunk, gathered, w_query, w_kv, cosine, sine, lengths, old)
        old = (k, v)
        keys.append(k)
        values.append(v)
        blocks = []
        for d in range(4):
            a = attended if d == 0 else shift(attended, "y", d)
            blocks += [a, swap(a)]
        parts = project_out(order, blocks, w_o)
        total = parts[0].astype(f32)
        for d in (1, 2, 3):
            total = total + shift(parts[d], "z", d).astype(f32)
        sums.append(total)
    mixed = (tokens.astype(f32) + jnp.concatenate(sums, axis=0)).astype(bf16)

    place = (y % 2) * 2 + c
    pair = jnp.stack(
        [
            lax.dynamic_slice(jnp.concatenate(part, axis=0), (place * 256, 0), (256, HEAD))
            for part in (keys, values)
        ]
    )
    pair = pair.reshape(2, 2, BLOCK, HEAD).transpose(1, 0, 2, 3)
    everyone = lax.all_gather(pair, ("z", "y", "c")).reshape(64, 2, BLOCK, HEAD)
    picked = pick_blocks(index, valid, everyone)
    arrived = jnp.stack([picked[0]] + [shift(picked[d], "g", d) for d in (1, 2, 3)])
    stored = jnp.stack(
        [lax.dynamic_index_in_dim(arrived, (g - s) % 4, 0, keepdims=False) for s in range(4)]
    )
    return mixed, stored[None]


def solution(mesh):
    grid = Mesh(mesh.devices.reshape(4, 4, 4, 2), ("g", "z", "y", "c"))
    tp = ("z", "y", "c")
    return jax.shard_map(
        local,
        mesh=grid,
        in_specs=(
            P("g", tp),
            P(tp),
            P(None, tp),
            P(None, None, tp),
            P(tp, None),
            P("g", None),
            P(),
        ),
        out_specs=(P("g", tp), P(("g",) + tp, None, None, None, None, None)),
        check_vma=False,
    )
```

```python
import functools
import math

import jax
import jax.numpy as jnp
from jax import lax
from jax.experimental import pallas as pl
from jax.experimental.pallas import tpu as pltpu
from jax.sharding import Mesh
from jax.sharding import PartitionSpec as P

WIDTH = 8192
HEAD = 128
BLOCK = 128
SEQ = 1024
COLS = 256
CHUNK = 512
ROPE_BASE = 500000.0
EPS = 1e-05
FILL = -1e30
SCORE_SCALE = math.log2(math.e) / math.sqrt(HEAD)
bf16 = jnp.bfloat16
f32 = jnp.float32

SHIFT = {d: [(i, (i + d) % 4) for i in range(4)] for d in (1, 2, 3)}
SWAP = [(0, 1), (1, 0)]
PAIR = [(0, 1), (1, 0), (2, 3), (3, 2)]


def shift(value, axis, distance):
    return lax.ppermute(value, axis, SHIFT[distance])


def swap(value):
    return lax.ppermute(value, "c", SWAP)


def rotate(vectors, cosine, sine):
    return vectors * cosine + pltpu.roll(vectors, HEAD // 2, 1) * sine


def scale_kernel(tokens, gain, sent):
    tok = tokens[...].astype(f32)
    sent[0:SEQ, :] = (tok * gain[...].astype(f32).reshape(1, COLS)).astype(bf16)
    diagonal = lax.broadcasted_iota(jnp.int32, (COLS, COLS), 0) == lax.broadcasted_iota(
        jnp.int32, (COLS, COLS), 1
    )
    rows = []
    for part in range(SEQ // COLS):
        here = tok[part * COLS : (part + 1) * COLS, :]
        column = jnp.sum(here * here, axis=1, keepdims=True)
        rows.append(jnp.sum(jnp.where(diagonal, column, 0.0), axis=0, keepdims=True))
    total = jnp.concatenate(rows + [jnp.zeros((4, COLS), f32)], axis=0)
    high = total.astype(bf16).astype(f32)
    sent[SEQ : SEQ + 16, :] = jnp.concatenate([high, total - high], axis=0).astype(bf16)


def scale_tokens(tokens, gain):
    return pl.pallas_call(
        scale_kernel,
        out_shape=jax.ShapeDtypeStruct((SEQ + 16, COLS), bf16),
        compiler_params=pltpu.CompilerParams(vmem_limit_bytes=56 << 20),
        name="scale_tokens",
    )(tokens, gain)


def row_factors(squares, part):
    diagonal = lax.broadcasted_iota(jnp.int32, (COLS, COLS), 0) == lax.broadcasted_iota(
        jnp.int32, (COLS, COLS), 1
    )
    every = jnp.sum(squares[...].astype(f32), axis=0)
    every = every[:8, :] + every[8:, :]
    mine = lax.broadcasted_iota(jnp.int32, (8, COLS), 0) == part
    total = jnp.sum(jnp.where(mine, every, 0.0), axis=0, keepdims=True)
    factor = lax.rsqrt(total * (1.0 / WIDTH) + EPS)
    return jnp.sum(jnp.where(diagonal, factor, 0.0), axis=1, keepdims=True)


def key_value_kernel(steps, per_step, place, x, squares, weights, cosine, sine, out, acc):
    step = pl.program_id(0)

    @pl.when(step == 0)
    def _():
        acc[...] = jnp.zeros_like(acc)

    rows = jnp.concatenate([x[i] for i in range(per_step)], axis=1)
    acc[...] += lax.dot_general(
        rows, weights[...], (((1,), (1,)), ((), ())), preferred_element_type=f32
    )

    @pl.when(step == steps - 1)
    def _():
        kv = (acc[...] * row_factors(squares, place[0])).astype(bf16)
        keys = rotate(kv[:, :HEAD].astype(f32), cosine[...], sine[...]).astype(bf16)
        for i in range(2):
            out[i, 0] = keys[i * BLOCK : (i + 1) * BLOCK, :]
            out[i, 1] = kv[i * BLOCK : (i + 1) * BLOCK, HEAD:]


def project_key_value(place, gathered, weights, cosine, sine):
    per_step = 8
    steps = 32 // per_step
    return pl.pallas_call(
        functools.partial(key_value_kernel, steps, per_step),
        grid_spec=pltpu.PrefetchScalarGridSpec(
            num_scalar_prefetch=1,
            grid=(steps,),
            in_specs=[
                pl.BlockSpec((per_step, COLS, COLS), lambda k, n: (k, n[0], 0)),
                pl.BlockSpec((32, 16, COLS), lambda k, n: (0, SEQ // 16, 0)),
                pl.BlockSpec((2 * HEAD, per_step * COLS), lambda k, n: (0, k)),
                pl.BlockSpec((COLS, HEAD), lambda k, n: (n[0], 0)),
                pl.BlockSpec((COLS, HEAD), lambda k, n: (n[0], 0)),
            ],
            out_specs=pl.BlockSpec((2, 2, BLOCK, HEAD), lambda k, n: (0, 0, 0, 0)),
            scratch_shapes=[pltpu.VMEM((COLS, 2 * HEAD), f32)],
        ),
        out_shape=jax.ShapeDtypeStruct((2, 2, BLOCK, HEAD), bf16),
        compiler_params=pltpu.CompilerParams(vmem_limit_bytes=56 << 20),
        cost_estimate=pl.CostEstimate(
            flops=2 * COLS * WIDTH * 256, bytes_accessed=8 << 20, transcendentals=0
        ),
        name="project_key_value",
    )(place, gathered, gathered, weights, cosine, sine)


def query_kernel(steps, per_step, x, squares, weights, cosine, sine, first, second, acc):
    step = pl.program_id(0)

    @pl.when(step == 0)
    def _():
        acc[...] = jnp.zeros_like(acc)

    rows = jnp.concatenate([x[i] for i in range(per_step)], axis=1)
    acc[...] += jnp.dot(rows, weights[...], preferred_element_type=f32)

    @pl.when(step == steps - 1)
    def _():
        for part in range(SEQ // COLS):
            here = pl.ds(part * COLS, COLS)
            q = acc[here, :] * row_factors(squares, part)
            c, s = cosine[here, :], sine[here, :]
            out = first if part < 2 else second
            out[pl.ds((part % 2) * COLS, COLS), :] = jnp.concatenate(
                [rotate(q[:, :HEAD], c, s), rotate(q[:, HEAD:], c, s)], axis=1
            ).astype(bf16)


def project_query(gathered, weights, cosine, sine):
    per_step = 8
    steps = 32 // per_step
    return pl.pallas_call(
        functools.partial(query_kernel, steps, per_step),
        grid=(steps,),
        in_specs=[
            pl.BlockSpec((per_step, SEQ, COLS), lambda k: (k, 0, 0)),
            pl.BlockSpec((32, 16, COLS), lambda k: (0, SEQ // 16, 0)),
            pl.BlockSpec((per_step * COLS, COLS), lambda k: (k, 0)),
            pl.BlockSpec((SEQ, HEAD), lambda k: (0, 0)),
            pl.BlockSpec((SEQ, HEAD), lambda k: (0, 0)),
        ],
        out_specs=[pl.BlockSpec((CHUNK, COLS), lambda k: (0, 0))] * 2,
        out_shape=[jax.ShapeDtypeStruct((CHUNK, COLS), bf16)] * 2,
        scratch_shapes=[pltpu.VMEM((SEQ, COLS), f32)],
        compiler_params=pltpu.CompilerParams(vmem_limit_bytes=56 << 20),
        cost_estimate=pl.CostEstimate(
            flops=2 * SEQ * WIDTH * 256, bytes_accessed=20 << 20, transcendentals=0
        ),
        name="project_query",
    )(gathered, gathered, weights, cosine, sine)


def attention_kernel(chunk, scalars, queries, kv0, kv1, kv2, kv3, attended, all_k, all_v):
    for source, kv in enumerate((kv0, kv1, kv2, kv3)):
        start = pl.multiple_of(scalars[4 + source] * 256, 256)
        for i in range(2):
            there = pl.ds(start + i * BLOCK, BLOCK)
            all_k[there, :] = kv[i, 0]
            all_v[there, :] = kv[i, 1]
    base = chunk * CHUNK
    for part in range(CHUNK // 256):
        first = base + part * 256
        low = max(0, first - 512)
        high = first + 256
        here = pl.ds(part * 256, 256)
        i = lax.broadcasted_iota(jnp.int32, (256, 1), 0) + first
        starts = jnp.zeros((256, 1), jnp.int32)
        end = jnp.int32(0)
        for doc in range(4):
            end = end + scalars[doc]
            starts = starts + jnp.where(i >= end, scalars[doc], 0)
        j = lax.broadcasted_iota(jnp.int32, (256, high - low), 1) + low
        allowed = (j <= i) & (j >= starts)
        k = all_k[low:high, :]
        v = all_v[low:high, :]
        outs = []
        for head in range(2):
            q = queries[here, head * HEAD : (head + 1) * HEAD]
            scores = lax.dot_general(q, k, (((1,), (1,)), ((), ())), preferred_element_type=f32)
            scores = jnp.where(allowed, scores * SCORE_SCALE, FILL)
            peak = jnp.max(scores, axis=1, keepdims=True)
            weights = jnp.exp2(scores - peak)
            norm = jnp.sum(weights, axis=1, keepdims=True)
            out = jnp.dot(weights.astype(bf16), v, preferred_element_type=f32)
            outs.append(out / norm)
        attended[here, :] = jnp.concatenate(outs, axis=1).astype(bf16)


def attend(chunk, scalars, queries, kvs):
    kv_spec = pl.BlockSpec((2, 2, BLOCK, HEAD), lambda k, n: (0, 0, 0, 0))
    return pl.pallas_call(
        functools.partial(attention_kernel, chunk),
        grid_spec=pltpu.PrefetchScalarGridSpec(
            num_scalar_prefetch=1,
            grid=(1,),
            in_specs=[pl.BlockSpec((CHUNK, COLS), lambda k, n: (0, 0))] + [kv_spec] * 4,
            out_specs=pl.BlockSpec((CHUNK, COLS), lambda k, n: (0, 0)),
            scratch_shapes=[pltpu.VMEM((SEQ, HEAD), bf16), pltpu.VMEM((SEQ, HEAD), bf16)],
        ),
        out_shape=jax.ShapeDtypeStruct((CHUNK, COLS), bf16),
        compiler_params=pltpu.CompilerParams(vmem_limit_bytes=56 << 20),
        cost_estimate=pl.CostEstimate(flops=1024, bytes_accessed=1024, transcendentals=0),
        name="attend",
    )(scalars, queries, *kvs)


def out_kernel(scalars, *refs):
    local, (up, far_up, far_down, down), blocks = refs[:4], refs[4:8], refs[8:12]
    keep, send = refs[12:14]
    rows = jnp.concatenate([b[...] for b in blocks], axis=1)
    half = 2 * COLS
    sources = (
        [(i * COLS, (i + 1) * COLS, w) for i, w in enumerate(local)],
        [(0, 4 * COLS, up)],
        [(0, half, far_up), (half, 4 * COLS, far_down)],
        [(0, 4 * COLS, down)],
    )
    for i, source in enumerate(sources):
        parts = [
            jnp.dot(rows[:, low:high], w[...], preferred_element_type=f32) for low, high, w in source
        ]
        part = functools.reduce(jnp.add, parts).astype(bf16)
        distance = scalars[i]
        mine, theirs = part[:, :COLS], part[:, COLS:]

        @pl.when(scalars[4] == 0)
        def _():
            keep[distance] = mine
            send[distance] = theirs

        @pl.when(scalars[4] == 1)
        def _():
            keep[distance] = theirs
            send[distance] = mine


def project_out(scalars, blocks, local, others):
    arrays = (*local, *others, *blocks)
    return pl.pallas_call(
        out_kernel,
        grid_spec=pltpu.PrefetchScalarGridSpec(
            num_scalar_prefetch=1,
            grid=(1,),
            in_specs=[pl.BlockSpec(a.shape, lambda i, n: (0, 0)) for a in arrays],
            out_specs=[pl.BlockSpec((4, CHUNK, COLS), lambda i, n: (0, 0, 0))] * 2,
        ),
        out_shape=[jax.ShapeDtypeStruct((4, CHUNK, COLS), bf16)] * 2,
        compiler_params=pltpu.CompilerParams(vmem_limit_bytes=56 << 20),
        cost_estimate=pl.CostEstimate(flops=1024, bytes_accessed=1024, transcendentals=0),
        name="project_out",
    )(scalars, *arrays)


def add_kernel(keep, got, *outs):
    for d in range(4):
        outs[d][...] = (keep[d].astype(f32) + got[d].astype(f32)).astype(bf16)


def add_cores(keep, got):
    return pl.pallas_call(
        add_kernel,
        out_shape=[jax.ShapeDtypeStruct((CHUNK, COLS), bf16)] * 4,
        compiler_params=pltpu.CompilerParams(vmem_limit_bytes=56 << 20),
        cost_estimate=pl.CostEstimate(flops=1024, bytes_accessed=1024, transcendentals=0),
        name="add_cores",
    )(keep, got)


def pick_kernel(index, valid, blocks, *rest):
    outs, sems = rest[:4], rest[4]

    def copy(i):
        return pltpu.make_async_copy(blocks.at[index[i]], outs[i // 2].at[i % 2], sems.at[i])

    for i in range(8):

        @pl.when(valid[i] > 0)
        def _():
            copy(i).start()

        @pl.when(valid[i] <= 0)
        def _():
            outs[i // 2][i % 2] = jnp.zeros((2, BLOCK, HEAD), bf16)

    for i in range(8):

        @pl.when(valid[i] > 0)
        def _():
            copy(i).wait()


def pick_blocks(index, valid, blocks):
    shape = (2, 2, BLOCK, HEAD)
    return pl.pallas_call(
        pick_kernel,
        grid_spec=pltpu.PrefetchScalarGridSpec(
            num_scalar_prefetch=2,
            grid=(1,),
            in_specs=[pl.BlockSpec(memory_space=pl.ANY)],
            out_specs=[pl.BlockSpec(shape, lambda i, n, m: (0, 0, 0, 0))] * 4,
            scratch_shapes=[pltpu.SemaphoreType.DMA((8,))],
        ),
        out_shape=[jax.ShapeDtypeStruct(shape, bf16)] * 4,
        compiler_params=pltpu.CompilerParams(vmem_limit_bytes=56 << 20),
        cost_estimate=pl.CostEstimate(flops=1024, bytes_accessed=1024, transcendentals=0),
        name="pick_blocks",
    )(index, valid, blocks)


def out_weights_along_y(w_out, g, y):
    def piece(d):
        column = (g * 8 + ((y + d) % 4) * 2) * COLS
        return lax.dynamic_slice(w_out, (0, column), (COLS, 2 * COLS))

    return [piece(0)] + [shift(piece(d), "y", d) for d in (1, 2, 3)]


def near_quarter(kv_weight, g):
    own = kv_weight.transpose(1, 2, 0)
    quarter = lax.dynamic_slice(own, (0, 0, g * 2048), (2, 32, 2048))
    return own, lax.ppermute(quarter, "y", PAIR)


def whole_near(near, g):
    relative = [near] + [shift(near, "g", d) for d in (3, 2, 1)]
    return lax.dynamic_slice(
        jnp.concatenate(relative + relative[:3], axis=2), (0, 0, ((4 - g) % 4) * 2048), (2, 32, WIDTH)
    )


def head_weights(own, near, y, c):
    pairs = []
    for value in (own, near):
        other = swap(value)
        pairs.append((jnp.where(c == 0, value, other), jnp.where(c == 0, other, value)))
    parts = [jnp.where(y % 2 == 0, pairs[0][i], pairs[1][i]) for i in range(2)]
    parts += [jnp.where(y % 2 == 0, pairs[1][i], pairs[0][i]) for i in range(2)]
    return jnp.stack(parts, axis=1).reshape(2 * HEAD, WIDTH)


def rope_tables(lengths):
    ends = jnp.cumsum(lengths)
    i = jnp.arange(SEQ, dtype=jnp.int32)
    passed = (i[:, None] >= ends[None, :]).astype(jnp.int32)
    positions = (i - jnp.sum(passed * lengths[None, :], axis=1)).astype(f32)
    frequency = jnp.exp(jnp.arange(HEAD // 2, dtype=f32) * (-2.0 * math.log(ROPE_BASE) / HEAD))
    angles = positions[:, None] * frequency[None, :]
    cosine, sine = jnp.cos(angles), jnp.sin(angles)
    return jnp.concatenate([cosine, cosine], 1), jnp.concatenate([-sine, sine], 1)


def store_plan(holder, g, z, y, c):
    owners = lax.dynamic_slice(holder[:, 0], (g * 64,), (64,))
    same = owners[:, None] == owners[None, :]
    before = jnp.arange(64)[None, :] < jnp.arange(64)[:, None]
    rank = jnp.sum((same & before).astype(jnp.int32), axis=1)
    slots = jnp.arange(64, dtype=jnp.int32)
    z_of, y_of, rest = slots // 16, (slots // 4) % 4, slots % 4
    block = ((y_of % 2) * 4 + rest) * 8 + z_of * 2 + y_of // 2
    owner, slot = owners[block], rank[block]
    target = (((g + jnp.arange(4)) % 4) * 32 + z * 8 + y * 2 + c).astype(jnp.int32)
    hit = (owner[None, None, :] == target[:, None, None]) & (
        slot[None, None, :] == jnp.arange(2)[None, :, None]
    )
    hit = hit.reshape(8, 64).astype(jnp.int32)
    return jnp.sum(hit * slots[None, :], axis=1), jnp.sum(hit, axis=1)


def local(tokens, norm_gain, w_query, kv_weight, w_out, doc_lengths, holder):
    g, z, y, c = (lax.axis_index(a) for a in ("g", "z", "y", "c"))
    sent = scale_tokens(tokens, norm_gain)
    gathered = lax.all_gather(sent, ("z", "y", "c"))

    own, near = near_quarter(kv_weight, g)
    local = out_weights_along_y(w_out, g, y)
    row = jnp.concatenate(local, axis=0)
    near, doc_lengths, holder, row = lax.optimization_barrier((near, doc_lengths, holder, row))
    up, down = shift(row, "g", 1), shift(row, "g", 3)
    far_up, far_down = shift(up[: 2 * COLS], "g", 1), shift(down[2 * COLS :], "g", 3)
    near = whole_near(near, g)
    w_kv = head_weights(own, near, y, c)
    order = jnp.stack([(g - z - d) % 4 for d in range(4)] + [c]).astype(jnp.int32)
    lengths = doc_lengths[0]
    cosine, sine = rope_tables(lengths)
    index, valid = store_plan(holder, g, z, y, c)
    low = y % 2
    place = low * 2 + c
    places = [place, low * 2 + 1 - c, (1 - low) * 2 + c, (1 - low) * 2 + 1 - c]
    scalars = jnp.concatenate([lengths, jnp.stack(places).astype(jnp.int32)])
    place = place.astype(jnp.int32).reshape(1)
    w_o = (local, (up, far_up, far_down, down))
    gathered, w_kv, w_o, order, index, valid, cosine, sine, scalars, place = (
        lax.optimization_barrier(
            (gathered, w_kv, w_o, order, index, valid, cosine, sine, scalars, place)
        )
    )

    own = project_key_value(place, gathered, w_kv, cosine, sine)
    everyone = lax.all_gather(own, ("z", "y", "c")).reshape(64, 2, BLOCK, HEAD)
    near = lax.ppermute(own, "y", PAIR)
    gathered, own = lax.optimization_barrier((gathered, own))
    queries = project_query(gathered, w_query, cosine, sine)
    near, queries = lax.optimization_barrier((near, queries))
    kvs = (own, swap(own), near, swap(near))

    attended = [attend(0, scalars, queries[0], kvs)]
    queries, attended[0] = lax.optimization_barrier((queries, attended[0]))
    attended.append(attend(1, scalars, queries[1], kvs))
    landed = [[shift(a, "y", d) for d in (1, 2, 3)] for a in attended]
    landed[0], attended[1] = lax.optimization_barrier((landed[0], attended[1]))
    sums = []
    for chunk in range(SEQ // CHUNK):
        keep, send = project_out(order, (attended[chunk], *landed[chunk]), *w_o)
        got = swap(send)
        if chunk == 0:
            keep, landed[1] = lax.optimization_barrier((keep, landed[1]))
        parts = add_cores(keep, got)
        sums.append([parts[0]] + [shift(parts[d], "z", d) for d in (1, 2, 3)])

    picked = pick_blocks(index, valid, everyone)
    arrived = [picked[0]] + [shift(picked[d], "g", d) for d in (1, 2, 3)]
    sums, arrived = lax.optimization_barrier((sums, arrived))
    sums = [sum(part.astype(f32) for part in moved) for moved in sums]
    mixed = (tokens.astype(f32) + jnp.concatenate(sums, axis=0)).astype(bf16)

    arrived = jnp.stack(arrived)
    stored = jnp.stack(
        [lax.dynamic_index_in_dim(arrived, (g - s) % 4, 0, keepdims=False) for s in range(4)]
    )
    return mixed, stored[None]


def solution(mesh):
    grid = Mesh(mesh.devices.reshape(4, 4, 4, 2), ("g", "z", "y", "c"))
    tp = ("z", "y", "c")
    return jax.shard_map(
        local,
        mesh=grid,
        in_specs=(
            P("g", tp),
            P(tp),
            P(None, tp),
            P(None, None, tp),
            P(tp, None),
            P("g", None),
            P(),
        ),
        out_specs=(P("g", tp), P(("g",) + tp, None, None, None, None, None)),
        check_vma=False,
    )
```

```python
import functools
import math

import jax
import jax.numpy as jnp
from jax import lax
from jax.experimental import pallas as pl
from jax.experimental.pallas import tpu as pltpu
from jax.sharding import Mesh
from jax.sharding import PartitionSpec as P

WIDTH = 8192
HEAD = 128
BLOCK = 128
SEQ = 1024
COLS = 256
CHUNK = 512
ROPE_BASE = 500000.0
EPS = 1e-05
FILL = -1e30
SCORE_SCALE = math.log2(math.e) / math.sqrt(HEAD)
bf16 = jnp.bfloat16
f32 = jnp.float32

SHIFT = {d: [(i, (i + d) % 4) for i in range(4)] for d in (1, 2, 3)}
SWAP = [(0, 1), (1, 0)]
PAIR = [(0, 1), (1, 0), (2, 3), (3, 2)]


def shift(value, axis, distance):
    return lax.ppermute(value, axis, SHIFT[distance])


def swap(value):
    return lax.ppermute(value, "c", SWAP)


def rotate(vectors, cosine, sine):
    return vectors * cosine + pltpu.roll(vectors, HEAD // 2, 1) * sine


def scale_kernel(tokens, gain, sent):
    tok = tokens[...].astype(f32)
    sent[0:SEQ, :] = (tok * gain[...].astype(f32).reshape(1, COLS)).astype(bf16)
    diagonal = lax.broadcasted_iota(jnp.int32, (COLS, COLS), 0) == lax.broadcasted_iota(
        jnp.int32, (COLS, COLS), 1
    )
    rows = []
    for part in range(SEQ // COLS):
        here = tok[part * COLS : (part + 1) * COLS, :]
        column = jnp.sum(here * here, axis=1, keepdims=True)
        rows.append(jnp.sum(jnp.where(diagonal, column, 0.0), axis=0, keepdims=True))
    total = jnp.concatenate(rows + [jnp.zeros((4, COLS), f32)], axis=0)
    high = total.astype(bf16).astype(f32)
    sent[SEQ : SEQ + 16, :] = jnp.concatenate([high, total - high], axis=0).astype(bf16)


def scale_tokens(tokens, gain):
    return pl.pallas_call(
        scale_kernel,
        out_shape=jax.ShapeDtypeStruct((SEQ + 16, COLS), bf16),
        compiler_params=pltpu.CompilerParams(vmem_limit_bytes=56 << 20),
        name="scale_tokens",
    )(tokens, gain)


def row_factors(squares, part):
    diagonal = lax.broadcasted_iota(jnp.int32, (COLS, COLS), 0) == lax.broadcasted_iota(
        jnp.int32, (COLS, COLS), 1
    )
    every = jnp.sum(squares[...].astype(f32), axis=0)
    every = every[:8, :] + every[8:, :]
    mine = lax.broadcasted_iota(jnp.int32, (8, COLS), 0) == part
    total = jnp.sum(jnp.where(mine, every, 0.0), axis=0, keepdims=True)
    factor = lax.rsqrt(total * (1.0 / WIDTH) + EPS)
    return jnp.sum(jnp.where(diagonal, factor, 0.0), axis=1, keepdims=True)


def key_value_kernel(steps, per_step, place, x, squares, weights, cosine, sine, out, acc):
    step = pl.program_id(0)

    @pl.when(step == 0)
    def _():
        acc[...] = jnp.zeros_like(acc)

    rows = jnp.concatenate([x[i] for i in range(per_step)], axis=1)
    acc[...] += lax.dot_general(
        rows, weights[...], (((1,), (1,)), ((), ())), preferred_element_type=f32
    )

    @pl.when(step == steps - 1)
    def _():
        kv = (acc[...] * row_factors(squares, place[0])).astype(bf16)
        keys = rotate(kv[:, :HEAD].astype(f32), cosine[...], sine[...]).astype(bf16)
        for i in range(2):
            out[i, 0] = keys[i * BLOCK : (i + 1) * BLOCK, :]
            out[i, 1] = kv[i * BLOCK : (i + 1) * BLOCK, HEAD:]


def project_key_value(place, gathered, weights, cosine, sine):
    per_step = 8
    steps = 32 // per_step
    return pl.pallas_call(
        functools.partial(key_value_kernel, steps, per_step),
        grid_spec=pltpu.PrefetchScalarGridSpec(
            num_scalar_prefetch=1,
            grid=(steps,),
            in_specs=[
                pl.BlockSpec((per_step, COLS, COLS), lambda k, n: (k, n[0], 0)),
                pl.BlockSpec((32, 16, COLS), lambda k, n: (0, SEQ // 16, 0)),
                pl.BlockSpec((2 * HEAD, per_step * COLS), lambda k, n: (0, k)),
                pl.BlockSpec((COLS, HEAD), lambda k, n: (n[0], 0)),
                pl.BlockSpec((COLS, HEAD), lambda k, n: (n[0], 0)),
            ],
            out_specs=pl.BlockSpec((2, 2, BLOCK, HEAD), lambda k, n: (0, 0, 0, 0)),
            scratch_shapes=[pltpu.VMEM((COLS, 2 * HEAD), f32)],
        ),
        out_shape=jax.ShapeDtypeStruct((2, 2, BLOCK, HEAD), bf16),
        compiler_params=pltpu.CompilerParams(vmem_limit_bytes=56 << 20),
        cost_estimate=pl.CostEstimate(
            flops=2 * COLS * WIDTH * 256, bytes_accessed=8 << 20, transcendentals=0
        ),
        name="project_key_value",
    )(place, gathered, gathered, weights, cosine, sine)


def query_kernel(chunk, steps, per_step, x, squares, weights, cosine, sine, out, acc):
    step = pl.program_id(0)

    @pl.when(step == 0)
    def _():
        acc[...] = jnp.zeros_like(acc)

    rows = jnp.concatenate([x[i] for i in range(per_step)], axis=1)
    acc[...] += jnp.dot(rows, weights[...], preferred_element_type=f32)

    @pl.when(step == steps - 1)
    def _():
        for part in range(CHUNK // COLS):
            here = pl.ds(part * COLS, COLS)
            q = acc[here, :] * row_factors(squares, chunk * (CHUNK // COLS) + part)
            c, s = cosine[here, :], sine[here, :]
            out[here, :] = jnp.concatenate(
                [rotate(q[:, :HEAD], c, s), rotate(q[:, HEAD:], c, s)], axis=1
            ).astype(bf16)


def project_query(chunk, gathered, weights, cosine, sine):
    per_step = 8
    steps = 32 // per_step
    return pl.pallas_call(
        functools.partial(query_kernel, chunk, steps, per_step),
        grid=(steps,),
        in_specs=[
            pl.BlockSpec((per_step, CHUNK, COLS), lambda k: (k, chunk, 0)),
            pl.BlockSpec((32, 16, COLS), lambda k: (0, SEQ // 16, 0)),
            pl.BlockSpec((per_step * COLS, COLS), lambda k: (k, 0)),
            pl.BlockSpec((CHUNK, HEAD), lambda k: (chunk, 0)),
            pl.BlockSpec((CHUNK, HEAD), lambda k: (chunk, 0)),
        ],
        out_specs=pl.BlockSpec((CHUNK, COLS), lambda k: (0, 0)),
        out_shape=jax.ShapeDtypeStruct((CHUNK, COLS), bf16),
        scratch_shapes=[pltpu.VMEM((CHUNK, COLS), f32)],
        compiler_params=pltpu.CompilerParams(vmem_limit_bytes=56 << 20),
        cost_estimate=pl.CostEstimate(
            flops=2 * CHUNK * WIDTH * 256, bytes_accessed=12 << 20, transcendentals=0
        ),
        name="project_query",
    )(gathered, gathered, weights, cosine, sine)


def attention_kernel(chunk, scalars, queries, kv0, kv1, kv2, kv3, attended, all_k, all_v):
    for source, kv in enumerate((kv0, kv1, kv2, kv3)):
        start = pl.multiple_of(scalars[4 + source] * 256, 256)
        for i in range(2):
            there = pl.ds(start + i * BLOCK, BLOCK)
            all_k[there, :] = kv[i, 0]
            all_v[there, :] = kv[i, 1]
    base = chunk * CHUNK
    for part in range(CHUNK // 256):
        first = base + part * 256
        low = max(0, first - 512)
        high = first + 256
        here = pl.ds(part * 256, 256)
        i = lax.broadcasted_iota(jnp.int32, (256, 1), 0) + first
        starts = jnp.zeros((256, 1), jnp.int32)
        end = jnp.int32(0)
        for doc in range(4):
            end = end + scalars[doc]
            starts = starts + jnp.where(i >= end, scalars[doc], 0)
        j = lax.broadcasted_iota(jnp.int32, (256, high - low), 1) + low
        allowed = (j <= i) & (j >= starts)
        k = all_k[low:high, :]
        v = all_v[low:high, :]
        outs = []
        for head in range(2):
            q = queries[here, head * HEAD : (head + 1) * HEAD]
            scores = lax.dot_general(q, k, (((1,), (1,)), ((), ())), preferred_element_type=f32)
            scores = jnp.where(allowed, scores * SCORE_SCALE, FILL)
            peak = jnp.max(scores, axis=1, keepdims=True)
            weights = jnp.exp2(scores - peak)
            norm = jnp.sum(weights, axis=1, keepdims=True)
            out = jnp.dot(weights.astype(bf16), v, preferred_element_type=f32)
            outs.append(out / norm)
        attended[here, :] = jnp.concatenate(outs, axis=1).astype(bf16)


def attend(chunk, scalars, queries, kvs):
    kv_spec = pl.BlockSpec((2, 2, BLOCK, HEAD), lambda k, n: (0, 0, 0, 0))
    return pl.pallas_call(
        functools.partial(attention_kernel, chunk),
        grid_spec=pltpu.PrefetchScalarGridSpec(
            num_scalar_prefetch=1,
            grid=(1,),
            in_specs=[pl.BlockSpec((CHUNK, COLS), lambda k, n: (0, 0))] + [kv_spec] * 4,
            out_specs=pl.BlockSpec((CHUNK, COLS), lambda k, n: (0, 0)),
            scratch_shapes=[pltpu.VMEM((SEQ, HEAD), bf16), pltpu.VMEM((SEQ, HEAD), bf16)],
        ),
        out_shape=jax.ShapeDtypeStruct((CHUNK, COLS), bf16),
        compiler_params=pltpu.CompilerParams(vmem_limit_bytes=56 << 20),
        cost_estimate=pl.CostEstimate(flops=1024, bytes_accessed=1024, transcendentals=0),
        name="attend",
    )(scalars, queries, *kvs)


def out_kernel(scalars, *refs):
    local, (up, far_up, far_down, down), blocks = refs[:4], refs[4:8], refs[8:12]
    keep, sends = refs[12], refs[13:]
    size = 4 // len(sends)
    rows = jnp.concatenate([b[...] for b in blocks], axis=1)
    half = 2 * COLS

    def put(distance, value):
        for j, send in enumerate(sends):

            @pl.when(distance // size == j)
            def _():
                send[distance % size] = value

    sources = (
        [(i * COLS, (i + 1) * COLS, w) for i, w in enumerate(local)],
        [(0, 4 * COLS, up)],
        [(0, half, far_up), (half, 4 * COLS, far_down)],
        [(0, 4 * COLS, down)],
    )
    for i, source in enumerate(sources):
        parts = [
            jnp.dot(rows[:, low:high], w[...], preferred_element_type=f32) for low, high, w in source
        ]
        part = functools.reduce(jnp.add, parts).astype(bf16)
        distance = scalars[i]
        mine, theirs = part[:, :COLS], part[:, COLS:]

        @pl.when(scalars[4] == 0)
        def _():
            keep[distance] = mine
            put(distance, theirs)

        @pl.when(scalars[4] == 1)
        def _():
            keep[distance] = theirs
            put(distance, mine)


def project_out(scalars, blocks, local, others):
    arrays = (*local, *others, *blocks)
    return pl.pallas_call(
        out_kernel,
        grid_spec=pltpu.PrefetchScalarGridSpec(
            num_scalar_prefetch=1,
            grid=(1,),
            in_specs=[pl.BlockSpec(a.shape, lambda i, n: (0, 0)) for a in arrays],
            out_specs=[pl.BlockSpec((4, CHUNK, COLS), lambda i, n: (0, 0, 0))]
            + [pl.BlockSpec((1, CHUNK, COLS), lambda i, n: (0, 0, 0))] * 4,
        ),
        out_shape=[jax.ShapeDtypeStruct((4, CHUNK, COLS), bf16)]
        + [jax.ShapeDtypeStruct((1, CHUNK, COLS), bf16)] * 4,
        compiler_params=pltpu.CompilerParams(vmem_limit_bytes=56 << 20),
        cost_estimate=pl.CostEstimate(flops=1024, bytes_accessed=1024, transcendentals=0),
        name="project_out",
    )(scalars, *arrays)


def add_kernel(keep, *refs):
    gots, outs = refs[:4], refs[4:]
    for d in range(4):
        got = gots[d // 1][d % 1]
        outs[d][...] = (keep[d].astype(f32) + got.astype(f32)).astype(bf16)


def add_cores(keep, got):
    return pl.pallas_call(
        add_kernel,
        out_shape=[jax.ShapeDtypeStruct((CHUNK, COLS), bf16)] * 4,
        compiler_params=pltpu.CompilerParams(vmem_limit_bytes=56 << 20),
        cost_estimate=pl.CostEstimate(flops=1024, bytes_accessed=1024, transcendentals=0),
        name="add_cores",
    )(keep, *got)


def pick_kernel(index, valid, blocks, *rest):
    outs, sems = rest[:4], rest[4]

    def copy(i):
        return pltpu.make_async_copy(blocks.at[index[i]], outs[i // 2].at[i % 2], sems.at[i])

    for i in range(8):

        @pl.when(valid[i] > 0)
        def _():
            copy(i).start()

        @pl.when(valid[i] <= 0)
        def _():
            outs[i // 2][i % 2] = jnp.zeros((2, BLOCK, HEAD), bf16)

    for i in range(8):

        @pl.when(valid[i] > 0)
        def _():
            copy(i).wait()


def pick_blocks(index, valid, blocks):
    shape = (2, 2, BLOCK, HEAD)
    return pl.pallas_call(
        pick_kernel,
        grid_spec=pltpu.PrefetchScalarGridSpec(
            num_scalar_prefetch=2,
            grid=(1,),
            in_specs=[pl.BlockSpec(memory_space=pl.ANY)],
            out_specs=[pl.BlockSpec(shape, lambda i, n, m: (0, 0, 0, 0))] * 4,
            scratch_shapes=[pltpu.SemaphoreType.DMA((8,))],
        ),
        out_shape=[jax.ShapeDtypeStruct(shape, bf16)] * 4,
        compiler_params=pltpu.CompilerParams(vmem_limit_bytes=56 << 20),
        cost_estimate=pl.CostEstimate(flops=1024, bytes_accessed=1024, transcendentals=0),
        name="pick_blocks",
    )(index, valid, blocks)


def out_weights_along(w_out, axis, place, stride, base):
    def piece(d):
        column = (base + ((place + d) % 4) * stride) * COLS
        return lax.dynamic_slice(w_out, (0, column), (COLS, 2 * COLS))

    return [piece(0)] + [shift(piece(d), axis, d) for d in (1, 2, 3)]


def near_quarter(kv_weight, g):
    own = kv_weight.transpose(1, 2, 0)
    quarter = lax.dynamic_slice(own, (0, 0, g * 2048), (2, 32, 2048))
    return own, lax.ppermute(quarter, "y", PAIR)


def whole_near(near, g):
    relative = [near] + [shift(near, "g", d) for d in (3, 2, 1)]
    return lax.dynamic_slice(
        jnp.concatenate(relative + relative[:3], axis=2), (0, 0, ((4 - g) % 4) * 2048), (2, 32, WIDTH)
    )


def head_weights(own, near, y, c):
    pairs = []
    for value in (own, near):
        other = swap(value)
        pairs.append((jnp.where(c == 0, value, other), jnp.where(c == 0, other, value)))
    parts = [jnp.where(y % 2 == 0, pairs[0][i], pairs[1][i]) for i in range(2)]
    parts += [jnp.where(y % 2 == 0, pairs[1][i], pairs[0][i]) for i in range(2)]
    return jnp.stack(parts, axis=1).reshape(2 * HEAD, WIDTH)


def rope_tables(lengths):
    ends = jnp.cumsum(lengths)
    i = jnp.arange(SEQ, dtype=jnp.int32)
    passed = (i[:, None] >= ends[None, :]).astype(jnp.int32)
    positions = (i - jnp.sum(passed * lengths[None, :], axis=1)).astype(f32)
    frequency = jnp.exp(jnp.arange(HEAD // 2, dtype=f32) * (-2.0 * math.log(ROPE_BASE) / HEAD))
    angles = positions[:, None] * frequency[None, :]
    cosine, sine = jnp.cos(angles), jnp.sin(angles)
    return jnp.concatenate([cosine, cosine], 1), jnp.concatenate([-sine, sine], 1)


def store_plan(holder, g, z, y, c):
    owners = lax.dynamic_slice(holder[:, 0], (g * 64,), (64,))
    same = owners[:, None] == owners[None, :]
    before = jnp.arange(64)[None, :] < jnp.arange(64)[:, None]
    rank = jnp.sum((same & before).astype(jnp.int32), axis=1)
    slots = jnp.arange(64, dtype=jnp.int32)
    z_of, y_of, rest = slots // 16, (slots // 4) % 4, slots % 4
    block = ((y_of % 2) * 4 + rest) * 8 + z_of * 2 + y_of // 2
    owner, slot = owners[block], rank[block]
    target = (((g + jnp.arange(4)) % 4) * 32 + z * 8 + y * 2 + c).astype(jnp.int32)
    hit = (owner[None, None, :] == target[:, None, None]) & (
        slot[None, None, :] == jnp.arange(2)[None, :, None]
    )
    hit = hit.reshape(8, 64).astype(jnp.int32)
    return jnp.sum(hit * slots[None, :], axis=1), jnp.sum(hit, axis=1)


def local(tokens, norm_gain, w_query, kv_weight, w_out, doc_lengths, holder):
    g, z, y, c = (lax.axis_index(a) for a in ("g", "z", "y", "c"))
    sent = scale_tokens(tokens, norm_gain)
    gathered = lax.all_gather(sent, ("z", "y", "c"))

    own, near = near_quarter(kv_weight, g)
    local = out_weights_along(w_out, "z", z, 8, g * 2)
    row = jnp.concatenate(local, axis=0)
    near, doc_lengths, holder, row = lax.optimization_barrier((near, doc_lengths, holder, row))
    up, down = shift(row, "g", 1), shift(row, "g", 3)
    far_up, far_down = shift(up[: 2 * COLS], "g", 1), shift(down[2 * COLS :], "g", 3)
    near = whole_near(near, g)
    w_kv = head_weights(own, near, y, c)
    order = jnp.stack([(g - y - d) % 4 for d in range(4)] + [c]).astype(jnp.int32)
    lengths = doc_lengths[0]
    cosine, sine = rope_tables(lengths)
    index, valid = store_plan(holder, g, z, y, c)
    low = y % 2
    place = low * 2 + c
    places = [place, low * 2 + 1 - c, (1 - low) * 2 + c, (1 - low) * 2 + 1 - c]
    scalars = jnp.concatenate([lengths, jnp.stack(places).astype(jnp.int32)])
    place = place.astype(jnp.int32).reshape(1)
    w_o = (local, (up, far_up, far_down, down))
    gathered, w_kv, w_o, order, index, valid, cosine, sine, scalars, place = (
        lax.optimization_barrier(
            (gathered, w_kv, w_o, order, index, valid, cosine, sine, scalars, place)
        )
    )

    own = project_key_value(place, gathered, w_kv, cosine, sine)
    everyone = lax.all_gather(own, ("z", "y", "c")).reshape(64, 2, BLOCK, HEAD)
    near = lax.ppermute(own, "y", PAIR)
    gathered, own = lax.optimization_barrier((gathered, own))
    queries = project_query(0, gathered, w_query, cosine, sine)
    near, queries = lax.optimization_barrier((near, queries))
    kvs = (own, swap(own), near, swap(near))
    attended = [attend(0, scalars, queries, kvs)]
    gathered, attended[0] = lax.optimization_barrier((gathered, attended[0]))
    queries = project_query(1, gathered, w_query, cosine, sine)
    attended.append(attend(1, scalars, queries, kvs))
    landed = [[shift(a, "z", d) for d in (1, 2, 3)] for a in attended]
    landed[0], attended[1] = lax.optimization_barrier((landed[0], attended[1]))
    picked = pick_blocks(index, valid, everyone)
    sums = []
    for chunk in range(SEQ // CHUNK):
        keep, *send = project_out(order, (attended[chunk], *landed[chunk]), *w_o)
        got = [swap(part) for part in send]
        if chunk == 0:
            got, landed[1] = lax.optimization_barrier((got, landed[1]))
        else:
            got, picked = lax.optimization_barrier((got, picked))
        parts = add_cores(keep, got)
        sums.append([parts[0]] + [shift(parts[d], "y", d) for d in (1, 2, 3)])

    arrived = [picked[0]] + [shift(picked[d], "g", d) for d in (1, 2, 3)]
    sums, arrived = lax.optimization_barrier((sums, arrived))
    sums = [sum(part.astype(f32) for part in moved) for moved in sums]
    mixed = (tokens.astype(f32) + jnp.concatenate(sums, axis=0)).astype(bf16)

    arrived = jnp.stack(arrived)
    stored = jnp.stack(
        [lax.dynamic_index_in_dim(arrived, (g - s) % 4, 0, keepdims=False) for s in range(4)]
    )
    return mixed, stored[None]


def solution(mesh):
    grid = Mesh(mesh.devices.reshape(4, 4, 4, 2), ("g", "z", "y", "c"))
    tp = ("z", "y", "c")
    return jax.shard_map(
        local,
        mesh=grid,
        in_specs=(
            P("g", tp),
            P(tp),
            P(None, tp),
            P(None, None, tp),
            P(tp, None),
            P("g", None),
            P(),
        ),
        out_specs=(P("g", tp), P(("g",) + tp, None, None, None, None, None)),
        check_vma=False,
    )
```

```python
import functools
import math

import jax
import jax.numpy as jnp
from jax import lax
from jax.experimental import pallas as pl
from jax.experimental.pallas import tpu as pltpu
from jax.sharding import Mesh
from jax.sharding import PartitionSpec as P

WIDTH = 8192
HEAD = 128
BLOCK = 128
SEQ = 1024
COLS = 256
CHUNK = 512
ROPE_BASE = 500000.0
EPS = 1e-05
FILL = -1e30
SCORE_SCALE = math.log2(math.e) / math.sqrt(HEAD)
bf16 = jnp.bfloat16
f32 = jnp.float32

SHIFT = {d: [(i, (i + d) % 4) for i in range(4)] for d in (1, 2, 3)}
SWAP = [(0, 1), (1, 0)]
PAIR = [(0, 1), (1, 0), (2, 3), (3, 2)]


def shift(value, axis, distance):
    return lax.ppermute(value, axis, SHIFT[distance])


def swap(value):
    return lax.ppermute(value, "c", SWAP)


def rotate(vectors, cosine, sine):
    return vectors * cosine + pltpu.roll(vectors, HEAD // 2, 1) * sine


def scale_kernel(tokens, gain, sent):
    tok = tokens[...].astype(f32)
    sent[0:SEQ, :] = (tok * gain[...].astype(f32).reshape(1, COLS)).astype(bf16)
    diagonal = lax.broadcasted_iota(jnp.int32, (COLS, COLS), 0) == lax.broadcasted_iota(
        jnp.int32, (COLS, COLS), 1
    )
    rows = []
    for part in range(SEQ // COLS):
        here = tok[part * COLS : (part + 1) * COLS, :]
        column = jnp.sum(here * here, axis=1, keepdims=True)
        rows.append(jnp.sum(jnp.where(diagonal, column, 0.0), axis=0, keepdims=True))
    total = jnp.concatenate(rows + [jnp.zeros((4, COLS), f32)], axis=0)
    high = total.astype(bf16).astype(f32)
    sent[SEQ : SEQ + 16, :] = jnp.concatenate([high, total - high], axis=0).astype(bf16)


def scale_tokens(tokens, gain):
    return pl.pallas_call(
        scale_kernel,
        out_shape=jax.ShapeDtypeStruct((SEQ + 16, COLS), bf16),
        compiler_params=pltpu.CompilerParams(vmem_limit_bytes=60 << 20),
        name="scale_tokens",
    )(tokens, gain)


def row_factors(squares, part):
    diagonal = lax.broadcasted_iota(jnp.int32, (COLS, COLS), 0) == lax.broadcasted_iota(
        jnp.int32, (COLS, COLS), 1
    )
    every = jnp.sum(squares[...].astype(f32), axis=0)
    every = every[:8, :] + every[8:, :]
    mine = lax.broadcasted_iota(jnp.int32, (8, COLS), 0) == part
    total = jnp.sum(jnp.where(mine, every, 0.0), axis=0, keepdims=True)
    factor = lax.rsqrt(total * (1.0 / WIDTH) + EPS)
    return jnp.sum(jnp.where(diagonal, factor, 0.0), axis=1, keepdims=True)


def key_value_kernel(steps, per_step, place, x, squares, weights, cosine, sine, out, acc):
    step = pl.program_id(0)

    @pl.when(step == 0)
    def _():
        acc[...] = jnp.zeros_like(acc)

    rows = jnp.concatenate([x[i] for i in range(per_step)], axis=1)
    acc[...] += lax.dot_general(
        rows, weights[...], (((1,), (1,)), ((), ())), preferred_element_type=f32
    )

    @pl.when(step == steps - 1)
    def _():
        kv = (acc[...] * row_factors(squares, place[0])).astype(bf16)
        keys = rotate(kv[:, :HEAD].astype(f32), cosine[...], sine[...]).astype(bf16)
        for i in range(2):
            out[i, 0] = keys[i * BLOCK : (i + 1) * BLOCK, :]
            out[i, 1] = kv[i * BLOCK : (i + 1) * BLOCK, HEAD:]


def project_key_value(place, gathered, weights, cosine, sine):
    per_step = 16
    steps = 32 // per_step
    return pl.pallas_call(
        functools.partial(key_value_kernel, steps, per_step),
        grid_spec=pltpu.PrefetchScalarGridSpec(
            num_scalar_prefetch=1,
            grid=(steps,),
            in_specs=[
                pl.BlockSpec((per_step, COLS, COLS), lambda k, n: (k, n[0], 0)),
                pl.BlockSpec((32, 16, COLS), lambda k, n: (0, SEQ // 16, 0)),
                pl.BlockSpec((2 * HEAD, per_step * COLS), lambda k, n: (0, k)),
                pl.BlockSpec((COLS, HEAD), lambda k, n: (n[0], 0)),
                pl.BlockSpec((COLS, HEAD), lambda k, n: (n[0], 0)),
            ],
            out_specs=pl.BlockSpec((2, 2, BLOCK, HEAD), lambda k, n: (0, 0, 0, 0)),
            scratch_shapes=[pltpu.VMEM((COLS, 2 * HEAD), f32)],
        ),
        out_shape=jax.ShapeDtypeStruct((2, 2, BLOCK, HEAD), bf16),
        compiler_params=pltpu.CompilerParams(vmem_limit_bytes=60 << 20),
        cost_estimate=pl.CostEstimate(
            flops=2 * COLS * WIDTH * 256, bytes_accessed=8 << 20, transcendentals=0
        ),
        name="project_key_value",
    )(place, gathered, gathered, weights, cosine, sine)


def query_kernel(chunk, steps, per_step, x, squares, weights, cosine, sine, out, acc):
    step = pl.program_id(0)

    @pl.when(step == 0)
    def _():
        acc[...] = jnp.zeros_like(acc)

    rows = jnp.concatenate([x[i] for i in range(per_step)], axis=1)
    acc[...] += jnp.dot(rows, weights[...], preferred_element_type=f32)

    @pl.when(step == steps - 1)
    def _():
        for part in range(CHUNK // COLS):
            here = pl.ds(part * COLS, COLS)
            q = acc[here, :] * row_factors(squares, chunk * (CHUNK // COLS) + part)
            c, s = cosine[here, :], sine[here, :]
            out[here, :] = jnp.concatenate(
                [rotate(q[:, :HEAD], c, s), rotate(q[:, HEAD:], c, s)], axis=1
            ).astype(bf16)


def project_query(chunk, gathered, weights, cosine, sine):
    per_step = 16
    steps = 32 // per_step
    return pl.pallas_call(
        functools.partial(query_kernel, chunk, steps, per_step),
        grid=(steps,),
        in_specs=[
            pl.BlockSpec((per_step, CHUNK, COLS), lambda k: (k, chunk, 0)),
            pl.BlockSpec((32, 16, COLS), lambda k: (0, SEQ // 16, 0)),
            pl.BlockSpec((per_step * COLS, COLS), lambda k: (k, 0)),
            pl.BlockSpec((CHUNK, HEAD), lambda k: (chunk, 0)),
            pl.BlockSpec((CHUNK, HEAD), lambda k: (chunk, 0)),
        ],
        out_specs=pl.BlockSpec((CHUNK, COLS), lambda k: (0, 0)),
        out_shape=jax.ShapeDtypeStruct((CHUNK, COLS), bf16),
        scratch_shapes=[pltpu.VMEM((CHUNK, COLS), f32)],
        compiler_params=pltpu.CompilerParams(vmem_limit_bytes=60 << 20),
        cost_estimate=pl.CostEstimate(
            flops=2 * CHUNK * WIDTH * 256, bytes_accessed=12 << 20, transcendentals=0
        ),
        name="project_query",
    )(gathered, gathered, weights, cosine, sine)


def attention_kernel(chunk, scalars, queries, kv0, kv1, kv2, kv3, attended, all_k, all_v):
    for source, kv in enumerate((kv0, kv1, kv2, kv3)):
        start = pl.multiple_of(scalars[4 + source] * 256, 256)
        for i in range(2):
            there = pl.ds(start + i * BLOCK, BLOCK)
            all_k[there, :] = kv[i, 0]
            all_v[there, :] = kv[i, 1]
    base = chunk * CHUNK
    for part in range(CHUNK // 256):
        first = base + part * 256
        low = max(0, first - 512)
        high = first + 256
        here = pl.ds(part * 256, 256)
        i = lax.broadcasted_iota(jnp.int32, (256, 1), 0) + first
        starts = jnp.zeros((256, 1), jnp.int32)
        end = jnp.int32(0)
        for doc in range(4):
            end = end + scalars[doc]
            starts = starts + jnp.where(i >= end, scalars[doc], 0)
        j = lax.broadcasted_iota(jnp.int32, (256, high - low), 1) + low
        allowed = (j <= i) & (j >= starts)
        k = all_k[low:high, :]
        v = all_v[low:high, :]
        outs = []
        for head in range(2):
            q = queries[here, head * HEAD : (head + 1) * HEAD]
            scores = lax.dot_general(q, k, (((1,), (1,)), ((), ())), preferred_element_type=f32)
            scores = jnp.where(allowed, scores * SCORE_SCALE, FILL)
            peak = jnp.max(scores, axis=1, keepdims=True)
            weights = jnp.exp2(scores - peak)
            norm = jnp.sum(weights, axis=1, keepdims=True)
            out = jnp.dot(weights.astype(bf16), v, preferred_element_type=f32)
            outs.append(out / norm)
        attended[here, :] = jnp.concatenate(outs, axis=1).astype(bf16)


def attend(chunk, scalars, queries, kvs):
    kv_spec = pl.BlockSpec((2, 2, BLOCK, HEAD), lambda k, n: (0, 0, 0, 0))
    return pl.pallas_call(
        functools.partial(attention_kernel, chunk),
        grid_spec=pltpu.PrefetchScalarGridSpec(
            num_scalar_prefetch=1,
            grid=(1,),
            in_specs=[pl.BlockSpec((CHUNK, COLS), lambda k, n: (0, 0))] + [kv_spec] * 4,
            out_specs=pl.BlockSpec((CHUNK, COLS), lambda k, n: (0, 0)),
            scratch_shapes=[pltpu.VMEM((SEQ, HEAD), bf16), pltpu.VMEM((SEQ, HEAD), bf16)],
        ),
        out_shape=jax.ShapeDtypeStruct((CHUNK, COLS), bf16),
        compiler_params=pltpu.CompilerParams(vmem_limit_bytes=60 << 20),
        cost_estimate=pl.CostEstimate(flops=1024, bytes_accessed=1024, transcendentals=0),
        name="attend",
    )(scalars, queries, *kvs)


def out_kernel(scalars, *refs):
    local, (up, far_up, far_down, down), blocks = refs[:4], refs[4:8], refs[8:12]
    keep, sends = refs[12], refs[13:]
    size = 4 // len(sends)
    rows = jnp.concatenate([b[...] for b in blocks], axis=1)
    half = 2 * COLS

    def put(distance, value):
        for j, send in enumerate(sends):

            @pl.when(distance // size == j)
            def _():
                send[distance % size] = value

    sources = (
        [(i * COLS, (i + 1) * COLS, w) for i, w in enumerate(local)],
        [(0, 4 * COLS, up)],
        [(0, half, far_up), (half, 4 * COLS, far_down)],
        [(0, 4 * COLS, down)],
    )
    for i, source in enumerate(sources):
        parts = [
            jnp.dot(rows[:, low:high], w[...], preferred_element_type=f32) for low, high, w in source
        ]
        part = functools.reduce(jnp.add, parts).astype(bf16)
        distance = scalars[i]
        mine, theirs = part[:, :COLS], part[:, COLS:]

        @pl.when(scalars[4] == 0)
        def _():
            keep[distance] = mine
            put(distance, theirs)

        @pl.when(scalars[4] == 1)
        def _():
            keep[distance] = theirs
            put(distance, mine)


def project_out(scalars, blocks, local, others):
    arrays = (*local, *others, *blocks)
    return pl.pallas_call(
        out_kernel,
        grid_spec=pltpu.PrefetchScalarGridSpec(
            num_scalar_prefetch=1,
            grid=(1,),
            in_specs=[pl.BlockSpec(a.shape, lambda i, n: (0, 0)) for a in arrays],
            out_specs=[pl.BlockSpec((4, CHUNK, COLS), lambda i, n: (0, 0, 0))]
            + [pl.BlockSpec((1, CHUNK, COLS), lambda i, n: (0, 0, 0))] * 4,
        ),
        out_shape=[jax.ShapeDtypeStruct((4, CHUNK, COLS), bf16)]
        + [jax.ShapeDtypeStruct((1, CHUNK, COLS), bf16)] * 4,
        compiler_params=pltpu.CompilerParams(vmem_limit_bytes=60 << 20),
        cost_estimate=pl.CostEstimate(flops=1024, bytes_accessed=1024, transcendentals=0),
        name="project_out",
    )(scalars, *arrays)


def add_kernel(keep, *refs):
    gots, outs = refs[:4], refs[4:]
    for d in range(4):
        got = gots[d // 1][d % 1]
        outs[d][...] = (keep[d].astype(f32) + got.astype(f32)).astype(bf16)


def add_cores(keep, got):
    return pl.pallas_call(
        add_kernel,
        out_shape=[jax.ShapeDtypeStruct((CHUNK, COLS), bf16)] * 4,
        compiler_params=pltpu.CompilerParams(vmem_limit_bytes=60 << 20),
        cost_estimate=pl.CostEstimate(flops=1024, bytes_accessed=1024, transcendentals=0),
        name="add_cores",
    )(keep, *got)


def pick_kernel(index, valid, blocks, *rest):
    outs, sems = rest[:4], rest[4]

    def copy(i):
        return pltpu.make_async_copy(blocks.at[index[i]], outs[i // 2].at[i % 2], sems.at[i])

    for i in range(8):

        @pl.when(valid[i] > 0)
        def _():
            copy(i).start()

        @pl.when(valid[i] <= 0)
        def _():
            outs[i // 2][i % 2] = jnp.zeros((2, BLOCK, HEAD), bf16)

    for i in range(8):

        @pl.when(valid[i] > 0)
        def _():
            copy(i).wait()


def pick_blocks(index, valid, blocks):
    shape = (2, 2, BLOCK, HEAD)
    return pl.pallas_call(
        pick_kernel,
        grid_spec=pltpu.PrefetchScalarGridSpec(
            num_scalar_prefetch=2,
            grid=(1,),
            in_specs=[pl.BlockSpec(memory_space=pl.ANY)],
            out_specs=[pl.BlockSpec(shape, lambda i, n, m: (0, 0, 0, 0))] * 4,
            scratch_shapes=[pltpu.SemaphoreType.DMA((8,))],
        ),
        out_shape=[jax.ShapeDtypeStruct(shape, bf16)] * 4,
        compiler_params=pltpu.CompilerParams(vmem_limit_bytes=60 << 20),
        cost_estimate=pl.CostEstimate(flops=1024, bytes_accessed=1024, transcendentals=0),
        name="pick_blocks",
    )(index, valid, blocks)


def out_weights_along(w_out, axis, place, stride, base):
    def piece(d):
        column = (base + ((place + d) % 4) * stride) * COLS
        return lax.dynamic_slice(w_out, (0, column), (COLS, 2 * COLS))

    return [piece(0)] + [shift(piece(d), axis, d) for d in (1, 2, 3)]


def near_quarter(kv_weight, g):
    own = kv_weight.transpose(1, 2, 0)
    quarter = lax.dynamic_slice(own, (0, 0, g * 2048), (2, 32, 2048))
    return own, lax.ppermute(quarter, "y", PAIR)


def whole_near(near, g):
    relative = [near] + [shift(near, "g", d) for d in (3, 2, 1)]
    return lax.dynamic_slice(
        jnp.concatenate(relative + relative[:3], axis=2), (0, 0, ((4 - g) % 4) * 2048), (2, 32, WIDTH)
    )


def head_weights(own, near, y, c):
    pairs = []
    for value in (own, near):
        other = swap(value)
        pairs.append((jnp.where(c == 0, value, other), jnp.where(c == 0, other, value)))
    parts = [jnp.where(y % 2 == 0, pairs[0][i], pairs[1][i]) for i in range(2)]
    parts += [jnp.where(y % 2 == 0, pairs[1][i], pairs[0][i]) for i in range(2)]
    return jnp.stack(parts, axis=1).reshape(2 * HEAD, WIDTH)


def rope_tables(lengths):
    ends = jnp.cumsum(lengths)
    i = jnp.arange(SEQ, dtype=jnp.int32)
    passed = (i[:, None] >= ends[None, :]).astype(jnp.int32)
    positions = (i - jnp.sum(passed * lengths[None, :], axis=1)).astype(f32)
    frequency = jnp.exp(jnp.arange(HEAD // 2, dtype=f32) * (-2.0 * math.log(ROPE_BASE) / HEAD))
    angles = positions[:, None] * frequency[None, :]
    cosine, sine = jnp.cos(angles), jnp.sin(angles)
    return jnp.concatenate([cosine, cosine], 1), jnp.concatenate([-sine, sine], 1)


def store_plan(holder, g, z, y, c):
    owners = lax.dynamic_slice(holder[:, 0], (g * 64,), (64,))
    same = owners[:, None] == owners[None, :]
    before = jnp.arange(64)[None, :] < jnp.arange(64)[:, None]
    rank = jnp.sum((same & before).astype(jnp.int32), axis=1)
    slots = jnp.arange(64, dtype=jnp.int32)
    z_of, y_of, rest = slots // 16, (slots // 4) % 4, slots % 4
    block = ((y_of % 2) * 4 + rest) * 8 + z_of * 2 + y_of // 2
    owner, slot = owners[block], rank[block]
    target = (((g + jnp.arange(4)) % 4) * 32 + z * 8 + y * 2 + c).astype(jnp.int32)
    hit = (owner[None, None, :] == target[:, None, None]) & (
        slot[None, None, :] == jnp.arange(2)[None, :, None]
    )
    hit = hit.reshape(8, 64).astype(jnp.int32)
    return jnp.sum(hit * slots[None, :], axis=1), jnp.sum(hit, axis=1)


def local(tokens, norm_gain, w_query, kv_weight, w_out, doc_lengths, holder):
    g, z, y, c = (lax.axis_index(a) for a in ("g", "z", "y", "c"))
    sent = scale_tokens(tokens, norm_gain)
    gathered = lax.all_gather(sent, ("z", "y", "c"))

    own, near = near_quarter(kv_weight, g)
    local = out_weights_along(w_out, "z", z, 8, g * 2)
    row = jnp.concatenate(local, axis=0)
    near, doc_lengths, holder, row = lax.optimization_barrier((near, doc_lengths, holder, row))
    up, down = shift(row, "g", 1), shift(row, "g", 3)
    far_up, far_down = shift(up[: 2 * COLS], "g", 1), shift(down[2 * COLS :], "g", 3)
    near = whole_near(near, g)
    w_kv = head_weights(own, near, y, c)
    order = jnp.stack([(g - y - d) % 4 for d in range(4)] + [c]).astype(jnp.int32)
    lengths = doc_lengths[0]
    cosine, sine = rope_tables(lengths)
    index, valid = store_plan(holder, g, z, y, c)
    low = y % 2
    place = low * 2 + c
    places = [place, low * 2 + 1 - c, (1 - low) * 2 + c, (1 - low) * 2 + 1 - c]
    scalars = jnp.concatenate([lengths, jnp.stack(places).astype(jnp.int32)])
    place = place.astype(jnp.int32).reshape(1)
    w_o = (local, (up, far_up, far_down, down))
    gathered, w_kv, w_o, order, index, valid, cosine, sine, scalars, place = (
        lax.optimization_barrier(
            (gathered, w_kv, w_o, order, index, valid, cosine, sine, scalars, place)
        )
    )

    own = project_key_value(place, gathered, w_kv, cosine, sine)
    everyone = lax.all_gather(own, ("z", "y", "c")).reshape(64, 2, BLOCK, HEAD)
    near = lax.ppermute(own, "y", PAIR)
    gathered, own = lax.optimization_barrier((gathered, own))
    queries = project_query(0, gathered, w_query, cosine, sine)
    near, queries = lax.optimization_barrier((near, queries))
    kvs = (own, swap(own), near, swap(near))
    attended = [attend(0, scalars, queries, kvs)]
    gathered, attended[0] = lax.optimization_barrier((gathered, attended[0]))
    queries = project_query(1, gathered, w_query, cosine, sine)
    attended.append(attend(1, scalars, queries, kvs))
    landed = [[shift(a, "z", d) for d in (1, 2, 3)] for a in attended]
    landed[0], attended[1] = lax.optimization_barrier((landed[0], attended[1]))
    picked = pick_blocks(index, valid, everyone)
    sums = []
    for chunk in range(SEQ // CHUNK):
        keep, *send = project_out(order, (attended[chunk], *landed[chunk]), *w_o)
        got = [swap(part) for part in send]
        if chunk == 0:
            got, landed[1] = lax.optimization_barrier((got, landed[1]))
        else:
            got, picked = lax.optimization_barrier((got, picked))
        parts = add_cores(keep, got)
        sums.append([parts[0]] + [shift(parts[d], "y", d) for d in (1, 2, 3)])

    arrived = [picked[0]] + [shift(picked[d], "g", d) for d in (1, 2, 3)]
    sums, arrived = lax.optimization_barrier((sums, arrived))
    sums = [sum(part.astype(f32) for part in moved) for moved in sums]
    mixed = (tokens.astype(f32) + jnp.concatenate(sums, axis=0)).astype(bf16)

    arrived = jnp.stack(arrived)
    stored = jnp.stack(
        [lax.dynamic_index_in_dim(arrived, (g - s) % 4, 0, keepdims=False) for s in range(4)]
    )
    return mixed, stored[None]


def solution(mesh):
    grid = Mesh(mesh.devices.reshape(4, 4, 4, 2), ("g", "z", "y", "c"))
    tp = ("z", "y", "c")
    return jax.shard_map(
        local,
        mesh=grid,
        in_specs=(
            P("g", tp),
            P(tp),
            P(None, tp),
            P(None, None, tp),
            P(tp, None),
            P("g", None),
            P(),
        ),
        out_specs=(P("g", tp), P(("g",) + tp, None, None, None, None, None)),
        check_vma=False,
    )
```

```python
import functools
import math

import jax
import jax.numpy as jnp
from jax import lax
from jax.experimental import pallas as pl
from jax.experimental.pallas import tpu as pltpu
from jax.sharding import Mesh
from jax.sharding import PartitionSpec as P

WIDTH = 8192
HEAD = 128
BLOCK = 128
SEQ = 1024
COLS = 256
CHUNK = 512
ROPE_BASE = 500000.0
EPS = 1e-05
FILL = -1e30
SCORE_SCALE = math.log2(math.e) / math.sqrt(HEAD)
bf16 = jnp.bfloat16
f32 = jnp.float32

SHIFT = {d: [(i, (i + d) % 4) for i in range(4)] for d in (1, 2, 3)}
SWAP = [(0, 1), (1, 0)]
PAIR = [(0, 1), (1, 0), (2, 3), (3, 2)]


def shift(value, axis, distance):
    return lax.ppermute(value, axis, SHIFT[distance])


def shift_all(values, axis):
    return [shift(values[d], axis, d) for d in (2, 1, 3)]


def swap(value):
    return lax.ppermute(value, "c", SWAP)


def rotate(vectors, cosine, sine):
    return vectors * cosine + pltpu.roll(vectors, HEAD // 2, 1) * sine


def scale_kernel(tokens, gain, sent):
    tok = tokens[...].astype(f32)
    sent[0:SEQ, :] = (tok * gain[...].astype(f32).reshape(1, COLS)).astype(bf16)
    diagonal = lax.broadcasted_iota(jnp.int32, (COLS, COLS), 0) == lax.broadcasted_iota(
        jnp.int32, (COLS, COLS), 1
    )
    rows = []
    for part in range(SEQ // COLS):
        here = tok[part * COLS : (part + 1) * COLS, :]
        column = jnp.sum(here * here, axis=1, keepdims=True)
        rows.append(jnp.sum(jnp.where(diagonal, column, 0.0), axis=0, keepdims=True))
    total = jnp.concatenate(rows + [jnp.zeros((4, COLS), f32)], axis=0)
    high = total.astype(bf16).astype(f32)
    sent[SEQ : SEQ + 16, :] = jnp.concatenate([high, total - high], axis=0).astype(bf16)


def scale_tokens(tokens, gain):
    return pl.pallas_call(
        scale_kernel,
        out_shape=jax.ShapeDtypeStruct((SEQ + 16, COLS), bf16),
        compiler_params=pltpu.CompilerParams(vmem_limit_bytes=60 << 20),
        name="scale_tokens",
    )(tokens, gain)


def row_factors(squares, part):
    diagonal = lax.broadcasted_iota(jnp.int32, (COLS, COLS), 0) == lax.broadcasted_iota(
        jnp.int32, (COLS, COLS), 1
    )
    every = jnp.sum(squares[...].astype(f32), axis=0)
    every = every[:8, :] + every[8:, :]
    mine = lax.broadcasted_iota(jnp.int32, (8, COLS), 0) == part
    total = jnp.sum(jnp.where(mine, every, 0.0), axis=0, keepdims=True)
    factor = lax.rsqrt(total * (1.0 / WIDTH) + EPS)
    return jnp.sum(jnp.where(diagonal, factor, 0.0), axis=1, keepdims=True)


def key_value_kernel(steps, per_step, place, x, squares, weights, cosine, sine, out, acc):
    step = pl.program_id(0)

    @pl.when(step == 0)
    def _():
        acc[...] = jnp.zeros_like(acc)

    rows = jnp.concatenate([x[i] for i in range(per_step)], axis=1)
    acc[...] += lax.dot_general(
        rows, weights[...], (((1,), (1,)), ((), ())), preferred_element_type=f32
    )

    @pl.when(step == steps - 1)
    def _():
        kv = (acc[...] * row_factors(squares, place[0])).astype(bf16)
        keys = rotate(kv[:, :HEAD].astype(f32), cosine[...], sine[...]).astype(bf16)
        for i in range(2):
            out[i, 0] = keys[i * BLOCK : (i + 1) * BLOCK, :]
            out[i, 1] = kv[i * BLOCK : (i + 1) * BLOCK, HEAD:]


def project_key_value(place, gathered, weights, cosine, sine):
    per_step = 16
    steps = 32 // per_step
    return pl.pallas_call(
        functools.partial(key_value_kernel, steps, per_step),
        grid_spec=pltpu.PrefetchScalarGridSpec(
            num_scalar_prefetch=1,
            grid=(steps,),
            in_specs=[
                pl.BlockSpec((per_step, COLS, COLS), lambda k, n: (k, n[0], 0)),
                pl.BlockSpec((32, 16, COLS), lambda k, n: (0, SEQ // 16, 0)),
                pl.BlockSpec((2 * HEAD, per_step * COLS), lambda k, n: (0, k)),
                pl.BlockSpec((COLS, HEAD), lambda k, n: (n[0], 0)),
                pl.BlockSpec((COLS, HEAD), lambda k, n: (n[0], 0)),
            ],
            out_specs=pl.BlockSpec((2, 2, BLOCK, HEAD), lambda k, n: (0, 0, 0, 0)),
            scratch_shapes=[pltpu.VMEM((COLS, 2 * HEAD), f32)],
        ),
        out_shape=jax.ShapeDtypeStruct((2, 2, BLOCK, HEAD), bf16),
        compiler_params=pltpu.CompilerParams(vmem_limit_bytes=60 << 20),
        cost_estimate=pl.CostEstimate(
            flops=2 * COLS * WIDTH * 256, bytes_accessed=8 << 20, transcendentals=0
        ),
        name="project_key_value",
    )(place, gathered, gathered, weights, cosine, sine)


def query_kernel(chunk, steps, per_step, x, squares, weights, cosine, sine, out, acc):
    step = pl.program_id(0)

    @pl.when(step == 0)
    def _():
        acc[...] = jnp.zeros_like(acc)

    rows = jnp.concatenate([x[i] for i in range(per_step)], axis=1)
    acc[...] += jnp.dot(rows, weights[...], preferred_element_type=f32)

    @pl.when(step == steps - 1)
    def _():
        for part in range(CHUNK // COLS):
            here = pl.ds(part * COLS, COLS)
            q = acc[here, :] * row_factors(squares, chunk * (CHUNK // COLS) + part)
            c, s = cosine[here, :], sine[here, :]
            out[here, :] = jnp.concatenate(
                [rotate(q[:, :HEAD], c, s), rotate(q[:, HEAD:], c, s)], axis=1
            ).astype(bf16)


def project_query(chunk, gathered, weights, cosine, sine):
    per_step = 16
    steps = 32 // per_step
    return pl.pallas_call(
        functools.partial(query_kernel, chunk, steps, per_step),
        grid=(steps,),
        in_specs=[
            pl.BlockSpec((per_step, CHUNK, COLS), lambda k: (k, chunk, 0)),
            pl.BlockSpec((32, 16, COLS), lambda k: (0, SEQ // 16, 0)),
            pl.BlockSpec((per_step * COLS, COLS), lambda k: (k, 0)),
            pl.BlockSpec((CHUNK, HEAD), lambda k: (chunk, 0)),
            pl.BlockSpec((CHUNK, HEAD), lambda k: (chunk, 0)),
        ],
        out_specs=pl.BlockSpec((CHUNK, COLS), lambda k: (0, 0)),
        out_shape=jax.ShapeDtypeStruct((CHUNK, COLS), bf16),
        scratch_shapes=[pltpu.VMEM((CHUNK, COLS), f32)],
        compiler_params=pltpu.CompilerParams(vmem_limit_bytes=60 << 20),
        cost_estimate=pl.CostEstimate(
            flops=2 * CHUNK * WIDTH * 256, bytes_accessed=12 << 20, transcendentals=0
        ),
        name="project_query",
    )(gathered, gathered, weights, cosine, sine)


def attention_kernel(chunk, scalars, queries, kv0, kv1, kv2, kv3, attended, all_k, all_v):
    for source, kv in enumerate((kv0, kv1, kv2, kv3)):
        start = pl.multiple_of(scalars[4 + source] * 256, 256)
        for i in range(2):
            there = pl.ds(start + i * BLOCK, BLOCK)
            all_k[there, :] = kv[i, 0]
            all_v[there, :] = kv[i, 1]
    base = chunk * CHUNK
    for part in range(CHUNK // 256):
        first = base + part * 256
        low = max(0, first - 512)
        high = first + 256
        here = pl.ds(part * 256, 256)
        i = lax.broadcasted_iota(jnp.int32, (256, 1), 0) + first
        starts = jnp.zeros((256, 1), jnp.int32)
        end = jnp.int32(0)
        for doc in range(4):
            end = end + scalars[doc]
            starts = starts + jnp.where(i >= end, scalars[doc], 0)
        j = lax.broadcasted_iota(jnp.int32, (256, high - low), 1) + low
        allowed = (j <= i) & (j >= starts)
        k = all_k[low:high, :]
        v = all_v[low:high, :]
        outs = []
        for head in range(2):
            q = queries[here, head * HEAD : (head + 1) * HEAD]
            scores = lax.dot_general(q, k, (((1,), (1,)), ((), ())), preferred_element_type=f32)
            scores = jnp.where(allowed, scores * SCORE_SCALE, FILL)
            peak = jnp.max(scores, axis=1, keepdims=True)
            weights = jnp.exp2(scores - peak)
            norm = jnp.sum(weights, axis=1, keepdims=True)
            out = jnp.dot(weights.astype(bf16), v, preferred_element_type=f32)
            outs.append(out / norm)
        attended[here, :] = jnp.concatenate(outs, axis=1).astype(bf16)


def attend(chunk, scalars, queries, kvs):
    kv_spec = pl.BlockSpec((2, 2, BLOCK, HEAD), lambda k, n: (0, 0, 0, 0))
    return pl.pallas_call(
        functools.partial(attention_kernel, chunk),
        grid_spec=pltpu.PrefetchScalarGridSpec(
            num_scalar_prefetch=1,
            grid=(1,),
            in_specs=[pl.BlockSpec((CHUNK, COLS), lambda k, n: (0, 0))] + [kv_spec] * 4,
            out_specs=pl.BlockSpec((CHUNK, COLS), lambda k, n: (0, 0)),
            scratch_shapes=[pltpu.VMEM((SEQ, HEAD), bf16), pltpu.VMEM((SEQ, HEAD), bf16)],
        ),
        out_shape=jax.ShapeDtypeStruct((CHUNK, COLS), bf16),
        compiler_params=pltpu.CompilerParams(vmem_limit_bytes=60 << 20),
        cost_estimate=pl.CostEstimate(flops=1024, bytes_accessed=1024, transcendentals=0),
        name="attend",
    )(scalars, queries, *kvs)


def out_kernel(scalars, *refs):
    local, (up, far_up, far_down, down), blocks = refs[:4], refs[4:8], refs[8:12]
    keep, sends = refs[12], refs[13:]
    size = 4 // len(sends)
    rows = jnp.concatenate([b[...] for b in blocks], axis=1)
    half = 2 * COLS

    def put(distance, value):
        for j, send in enumerate(sends):

            @pl.when(distance // size == j)
            def _():
                send[distance % size] = value

    sources = (
        [(i * COLS, (i + 1) * COLS, w) for i, w in enumerate(local)],
        [(0, 4 * COLS, up)],
        [(0, half, far_up), (half, 4 * COLS, far_down)],
        [(0, 4 * COLS, down)],
    )
    for i, source in enumerate(sources):
        parts = [
            jnp.dot(rows[:, low:high], w[...], preferred_element_type=f32) for low, high, w in source
        ]
        part = functools.reduce(jnp.add, parts).astype(bf16)
        distance = scalars[i]
        mine, theirs = part[:, :COLS], part[:, COLS:]

        @pl.when(scalars[4] == 0)
        def _():
            keep[distance] = mine
            put(distance, theirs)

        @pl.when(scalars[4] == 1)
        def _():
            keep[distance] = theirs
            put(distance, mine)


def project_out(scalars, blocks, local, others):
    arrays = (*local, *others, *blocks)
    return pl.pallas_call(
        out_kernel,
        grid_spec=pltpu.PrefetchScalarGridSpec(
            num_scalar_prefetch=1,
            grid=(1,),
            in_specs=[pl.BlockSpec(a.shape, lambda i, n: (0, 0)) for a in arrays],
            out_specs=[pl.BlockSpec((4, CHUNK, COLS), lambda i, n: (0, 0, 0))]
            + [pl.BlockSpec((1, CHUNK, COLS), lambda i, n: (0, 0, 0))] * 4,
        ),
        out_shape=[jax.ShapeDtypeStruct((4, CHUNK, COLS), bf16)]
        + [jax.ShapeDtypeStruct((1, CHUNK, COLS), bf16)] * 4,
        compiler_params=pltpu.CompilerParams(vmem_limit_bytes=60 << 20),
        cost_estimate=pl.CostEstimate(flops=1024, bytes_accessed=1024, transcendentals=0),
        name="project_out",
    )(scalars, *arrays)


def add_kernel(keep, *refs):
    gots, outs = refs[:4], refs[4:]
    for d in range(4):
        got = gots[d // 1][d % 1]
        outs[d][...] = (keep[d].astype(f32) + got.astype(f32)).astype(bf16)


def add_cores(keep, got):
    return pl.pallas_call(
        add_kernel,
        out_shape=[jax.ShapeDtypeStruct((CHUNK, COLS), bf16)] * 4,
        compiler_params=pltpu.CompilerParams(vmem_limit_bytes=60 << 20),
        cost_estimate=pl.CostEstimate(flops=1024, bytes_accessed=1024, transcendentals=0),
        name="add_cores",
    )(keep, *got)


def pick_kernel(index, valid, blocks, *rest):
    outs, sems = rest[:4], rest[4]

    def copy(i):
        return pltpu.make_async_copy(blocks.at[index[i]], outs[i // 2].at[i % 2], sems.at[i])

    for i in range(8):

        @pl.when(valid[i] > 0)
        def _():
            copy(i).start()

        @pl.when(valid[i] <= 0)
        def _():
            outs[i // 2][i % 2] = jnp.zeros((2, BLOCK, HEAD), bf16)

    for i in range(8):

        @pl.when(valid[i] > 0)
        def _():
            copy(i).wait()


def pick_blocks(index, valid, blocks):
    shape = (2, 2, BLOCK, HEAD)
    return pl.pallas_call(
        pick_kernel,
        grid_spec=pltpu.PrefetchScalarGridSpec(
            num_scalar_prefetch=2,
            grid=(1,),
            in_specs=[pl.BlockSpec(memory_space=pl.ANY)],
            out_specs=[pl.BlockSpec(shape, lambda i, n, m: (0, 0, 0, 0))] * 4,
            scratch_shapes=[pltpu.SemaphoreType.DMA((8,))],
        ),
        out_shape=[jax.ShapeDtypeStruct(shape, bf16)] * 4,
        compiler_params=pltpu.CompilerParams(vmem_limit_bytes=60 << 20),
        cost_estimate=pl.CostEstimate(flops=1024, bytes_accessed=1024, transcendentals=0),
        name="pick_blocks",
    )(index, valid, blocks)


def out_weights_along(w_out, axis, place, stride, base):
    def piece(d):
        column = (base + ((place + d) % 4) * stride) * COLS
        return lax.dynamic_slice(w_out, (0, column), (COLS, 2 * COLS))

    return [piece(0)] + [shift(piece(d), axis, d) for d in (1, 2, 3)]


def near_quarter(kv_weight, g):
    own = kv_weight.transpose(1, 2, 0)
    quarter = lax.dynamic_slice(own, (0, 0, g * 2048), (2, 32, 2048))
    return own, lax.ppermute(quarter, "y", PAIR)


def whole_near(near, g):
    relative = [near] + [shift(near, "g", d) for d in (3, 2, 1)]
    return lax.dynamic_slice(
        jnp.concatenate(relative + relative[:3], axis=2), (0, 0, ((4 - g) % 4) * 2048), (2, 32, WIDTH)
    )


def head_weights(own, near, y, c):
    pairs = []
    for value in (own, near):
        other = swap(value)
        pairs.append((jnp.where(c == 0, value, other), jnp.where(c == 0, other, value)))
    parts = [jnp.where(y % 2 == 0, pairs[0][i], pairs[1][i]) for i in range(2)]
    parts += [jnp.where(y % 2 == 0, pairs[1][i], pairs[0][i]) for i in range(2)]
    return jnp.stack(parts, axis=1).reshape(2 * HEAD, WIDTH)


def rope_tables(lengths):
    ends = jnp.cumsum(lengths)
    i = jnp.arange(SEQ, dtype=jnp.int32)
    passed = (i[:, None] >= ends[None, :]).astype(jnp.int32)
    positions = (i - jnp.sum(passed * lengths[None, :], axis=1)).astype(f32)
    frequency = jnp.exp(jnp.arange(HEAD // 2, dtype=f32) * (-2.0 * math.log(ROPE_BASE) / HEAD))
    angles = positions[:, None] * frequency[None, :]
    cosine, sine = jnp.cos(angles), jnp.sin(angles)
    return jnp.concatenate([cosine, cosine], 1), jnp.concatenate([-sine, sine], 1)


def store_plan(holder, g, z, y, c):
    owners = lax.dynamic_slice(holder[:, 0], (g * 64,), (64,))
    same = owners[:, None] == owners[None, :]
    before = jnp.arange(64)[None, :] < jnp.arange(64)[:, None]
    rank = jnp.sum((same & before).astype(jnp.int32), axis=1)
    slots = jnp.arange(64, dtype=jnp.int32)
    y_of, z_of, rest = slots // 16, (slots // 4) % 4, slots % 4
    block = ((y_of % 2) * 4 + rest) * 8 + z_of * 2 + y_of // 2
    owner, slot = owners[block], rank[block]
    target = (((g + jnp.arange(4)) % 4) * 32 + z * 8 + y * 2 + c).astype(jnp.int32)
    hit = (owner[None, None, :] == target[:, None, None]) & (
        slot[None, None, :] == jnp.arange(2)[None, :, None]
    )
    hit = hit.reshape(8, 64).astype(jnp.int32)
    return jnp.sum(hit * slots[None, :], axis=1), jnp.sum(hit, axis=1)


def local(tokens, norm_gain, w_query, kv_weight, w_out, doc_lengths, holder):
    g, z, y, c = (lax.axis_index(a) for a in ("g", "z", "y", "c"))
    sent = scale_tokens(tokens, norm_gain)
    gathered = lax.all_gather(sent, ("z", "y", "c"))

    own, near = near_quarter(kv_weight, g)
    local = out_weights_along(w_out, "z", z, 8, g * 2)
    row = jnp.concatenate(local, axis=0)
    near, doc_lengths, holder, row = lax.optimization_barrier((near, doc_lengths, holder, row))
    up, down = shift(row, "g", 1), shift(row, "g", 3)
    far_up, far_down = shift(up[: 2 * COLS], "g", 1), shift(down[2 * COLS :], "g", 3)
    near = whole_near(near, g)
    w_kv = head_weights(own, near, y, c)
    order = jnp.stack([(g - y - d) % 4 for d in range(4)] + [c]).astype(jnp.int32)
    lengths = doc_lengths[0]
    cosine, sine = rope_tables(lengths)
    index, valid = store_plan(holder, g, z, y, c)
    low = y % 2
    place = low * 2 + c
    places = [place, low * 2 + 1 - c, (1 - low) * 2 + c, (1 - low) * 2 + 1 - c]
    scalars = jnp.concatenate([lengths, jnp.stack(places).astype(jnp.int32)])
    place = place.astype(jnp.int32).reshape(1)
    w_o = (local, (up, far_up, far_down, down))
    gathered, w_kv, w_o, order, index, valid, cosine, sine, scalars, place = (
        lax.optimization_barrier(
            (gathered, w_kv, w_o, order, index, valid, cosine, sine, scalars, place)
        )
    )

    own = project_key_value(place, gathered, w_kv, cosine, sine)
    everyone = lax.all_gather(own, ("y", "z", "c")).reshape(64, 2, BLOCK, HEAD)
    near = lax.ppermute(own, "y", PAIR)
    gathered, own = lax.optimization_barrier((gathered, own))
    queries = project_query(0, gathered, w_query, cosine, sine)
    near, queries = lax.optimization_barrier((near, queries))
    kvs = (own, swap(own), near, swap(near))
    attended = [attend(0, scalars, queries, kvs)]
    gathered, attended[0] = lax.optimization_barrier((gathered, attended[0]))
    queries = project_query(1, gathered, w_query, cosine, sine)
    attended.append(attend(1, scalars, queries, kvs))
    landed = [shift_all([a] * 4, "z") for a in attended]
    landed[0], attended[1] = lax.optimization_barrier((landed[0], attended[1]))
    picked = pick_blocks(index, valid, everyone)
    sums = []
    for chunk in range(SEQ // CHUNK):
        keep, *send = project_out(order, (attended[chunk], *(landed[chunk][i] for i in (1, 0, 2))), *w_o)
        got = [swap(part) for part in send]
        if chunk == 0:
            got, landed[1] = lax.optimization_barrier((got, landed[1]))
        else:
            got, picked = lax.optimization_barrier((got, picked))
        parts = add_cores(keep, got)
        sums.append([parts[0]] + shift_all(parts, "y"))

    arrived = [picked[0]] + [shift(picked[d], "g", d) for d in (1, 2, 3)]
    sums, arrived = lax.optimization_barrier((sums, arrived))
    sums = [sum(part.astype(f32) for part in moved) for moved in sums]
    mixed = (tokens.astype(f32) + jnp.concatenate(sums, axis=0)).astype(bf16)

    arrived = jnp.stack(arrived)
    stored = jnp.stack(
        [lax.dynamic_index_in_dim(arrived, (g - s) % 4, 0, keepdims=False) for s in range(4)]
    )
    return mixed, stored[None]


def solution(mesh):
    grid = Mesh(mesh.devices.reshape(4, 4, 4, 2), ("g", "z", "y", "c"))
    tp = ("z", "y", "c")
    return jax.shard_map(
        local,
        mesh=grid,
        in_specs=(
            P("g", tp),
            P(tp),
            P(None, tp),
            P(None, None, tp),
            P(tp, None),
            P("g", None),
            P(),
        ),
        out_specs=(P("g", tp), P(("g",) + tp, None, None, None, None, None)),
        check_vma=False,
    )
```
